32 devices in a mesh: group: 2 (over y), expert: 4 (over z), dp: 4 (over x, core).
Axes of the slice: x: 2, y: 2, z: 4, core: 2. Of those that a mesh axis runs over, the one named last changes fastest.
Arguments:
- tokens: bfloat16 [4096, 2048], P(('group', 'expert', 'dp')), parts along dimension 0, may hold values from -6 to 6
- cotangent: bfloat16 [4096, 2048], P(('group', 'expert', 'dp')), parts along dimension 0, may hold values from -4 to 4
- expert_ids: int32 [4096, 8], P(('group', 'expert', 'dp')), parts along dimension 0, may hold values from 0 to 15, as said below
- gates: bfloat16 [4096, 8], P(('group', 'expert', 'dp')), parts along dimension 0, may hold values from 0.029907227 to 0.5
- w_gate: bfloat16 [16, 2048, 384], P(('expert', 'dp')), may hold values from -0.125 to 0.125
- w_up: bfloat16 [16, 2048, 384], P(('expert', 'dp')), may hold values from -0.125 to 0.125
- w_down: bfloat16 [16, 384, 2048], P(('expert', 'dp')), may hold values from -0.3125 to 0.3125
Outputs:
- tokens_grad: bfloat16 [4096, 2048], P(('group', 'expert', 'dp')), parts along dimension 0
- gates_grad: bfloat16 [4096, 8], P(('group', 'expert', 'dp')), parts along dimension 0
- grad_gate: bfloat16 [32, 2048, 384], P(('group', 'expert', 'dp')), parts along dimension 0
- grad_up: bfloat16 [32, 2048, 384], P(('group', 'expert', 'dp')), parts along dimension 0
- grad_down: bfloat16 [32, 384, 2048], P(('group', 'expert', 'dp')), parts along dimension 0
The draws below stay inside these ranges and needn't reach their ends.
There are 2 independent parts, one for each index of `group`. The reference program is written for one: setup_inputs(seed, part) draws one part's arguments, and reference() takes and returns one part's arrays. A program takes and returns all parts, laid end to end along the dimension named above; an argument that names none is the same for every part. Nothing has to cross between parts.
Inputs may be any that keep to these rules, and one draw needn't show every extreme that they name: `expert_ids`: each row names 8 different experts; the 128 rows of one device (aligned blocks) name every expert exactly 128 * 8 // 16 times.
All inputs are finite; a program needn't handle non-finite values.
Results may differ from the reference program's by a relative error of at most 0.0085.
Values may be sent and summed in bfloat16 or wider, within the bound.
No kernel may reach another device: no remote copies, remote signals or barrier semaphores. Data moves between devices by JAX's collectives and lax.ppermute only.
A program may use at most 128 MiB of HBM per device.

```python
import math
import jax
import jax.numpy as jnp
from jax import lax

D = 2048
FF = 384
TOPK = 8
TOK_DEV = 128
EXPERTS = 16
TOKENS = 2048


def draw_expert_ids(key, part):
    key = jax.random.fold_in(key, 11)
    block_count = TOKENS // TOK_DEV

    def one_block(block_key):
        keys = jax.random.split(block_key, 3)
        token_perm = jax.random.permutation(keys[0], TOK_DEV)
        expert_perm = jax.random.permutation(keys[1], EXPERTS)
        offset = jax.random.randint(keys[2], (TOK_DEV, 1), 0, TOPK)
        column = (jnp.arange(TOPK, dtype=jnp.int32)[None, :] + offset) % TOPK
        base = token_perm[:, None] * TOPK + column
        return expert_perm[base % EXPERTS]
    chosen = jax.vmap(one_block)(jax.random.split(key, block_count))
    return chosen.reshape(TOKENS, TOPK).astype(jnp.int32)


def level_of(stream_key, shape, shards, smallest, largest):
    def one(dim, parts):
        steps = jax.random.uniform(jax.random.fold_in(jax.random.fold_in(stream_key, 6), dim), (parts,), jnp.float32, smallest / len(shards), largest / len(shards))
        return jnp.repeat(jnp.exp(steps), shape[dim] // parts).reshape((-1,) + (1,) * (len(shape) - dim - 1))

    gain = one(*shards[0])
    for cut in shards[1:]:
        gain = gain * one(*cut)
    return gain


def normal_values(own_key, dims, width, limit, shards=(), kind=jnp.bfloat16):
    values = jax.random.normal(own_key, dims, jnp.float32) * width
    if len(shards) > 0:
        values = level_of(own_key, dims, shards, -0.22, 0.18) * values
    return jnp.clip(values, min=-limit, max=limit).astype(kind)


def setup_inputs(seed: int = 0, part: int = 0) -> dict:
    key_list = jax.random.split(jax.random.key(seed), 8)
    own_keys = jax.random.split(jax.random.fold_in(key_list[7], part), 8)
    return {
        "tokens": normal_values(own_keys[0], (TOKENS, D), 1.0, 6.0, ((0, 16),)),
        "cotangent": normal_values(own_keys[1], (TOKENS, D), 0.5, 4.0, ((0, 16),)),
        "expert_ids": draw_expert_ids(jax.random.fold_in(jax.random.fold_in(key_list[7], part), 71), part),
        "gates": jnp.clip(jnp.exp(math.log(0.5) - 2.816508 * jax.random.uniform(own_keys[3], (TOKENS, TOPK), jnp.float32) ** level_of(own_keys[3], (TOKENS, TOPK), ((0, 16),), -0.2, 0.2)), 0.029907227, 0.5).astype(jnp.bfloat16),
        "w_gate": normal_values(key_list[4], (EXPERTS, D, FF), D ** -0.5, 0.125, ((0, 16),)),
        "w_up": normal_values(key_list[5], (EXPERTS, D, FF), D ** -0.5, 0.125, ((0, 16),)),
        "w_down": normal_values(key_list[6], (EXPERTS, FF, D), FF ** -0.5, 0.3125, ((0, 16),)),
    }


def expert_backward(rows_in, rows_cot, row_gate, w_one, u_one, d_one):
    pre_gate = jnp.dot(rows_in, w_one, preferred_element_type=jnp.float32)
    pre_up = jnp.dot(rows_in, u_one, preferred_element_type=jnp.float32)
    sigma = jax.nn.sigmoid(pre_gate)
    active = pre_gate * sigma
    hidden = (active * pre_up).astype(jnp.bfloat16)
    back_hidden = jnp.dot(rows_cot, d_one.T, preferred_element_type=jnp.float32)
    gate_term = jnp.sum(hidden.astype(jnp.float32) * back_hidden, axis=1).astype(jnp.bfloat16)
    weight_col = row_gate.astype(jnp.float32)[:, None]
    scaled_back = weight_col * back_hidden
    grad_pre_gate = (scaled_back * pre_up * sigma * (1.0 + pre_gate * (1.0 - sigma))).astype(jnp.bfloat16)
    grad_pre_up = (scaled_back * active).astype(jnp.bfloat16)
    scaled_hidden = (weight_col * active * pre_up).astype(jnp.bfloat16)
    row_grad = (jnp.dot(grad_pre_gate, w_one.T, preferred_element_type=jnp.float32)
                + jnp.dot(grad_pre_up, u_one.T, preferred_element_type=jnp.float32)).astype(jnp.bfloat16)
    grad_w_gate = jnp.dot(rows_in.T, grad_pre_gate, preferred_element_type=jnp.float32).astype(jnp.bfloat16)
    grad_w_up = jnp.dot(rows_in.T, grad_pre_up, preferred_element_type=jnp.float32).astype(jnp.bfloat16)
    grad_w_down = jnp.dot(scaled_hidden.T, rows_cot, preferred_element_type=jnp.float32).astype(jnp.bfloat16)
    return row_grad, gate_term, grad_w_gate, grad_w_up, grad_w_down


def reference(tokens, cotangent, expert_ids, gates, w_gate, w_up, w_down):
    assigned = TOKENS * TOPK
    per_expert = assigned // EXPERTS
    position = jnp.arange(assigned, dtype=jnp.int32)
    order = jnp.argsort(expert_ids.reshape(-1) * assigned + position).astype(jnp.int32)
    blocks = order.reshape(EXPERTS, per_expert)
    flat_gates = gates.reshape(-1)

    def advance(carry, inputs):
        total_grad, total_gate = carry
        picks, w_one, u_one, d_one = inputs
        source = (picks // TOPK).astype(jnp.int32)
        results = expert_backward(tokens[source], cotangent[source], flat_gates[picks], w_one, u_one, d_one)
        total_grad = total_grad.at[source].add(results[0].astype(jnp.float32))
        total_gate = total_gate.at[picks].set(results[1])
        return (total_grad, total_gate), (results[2], results[3], results[4])

    start = (jnp.zeros((TOKENS, D), jnp.float32), jnp.zeros((assigned,), jnp.bfloat16))
    (total_grad, total_gate), grads = lax.scan(advance, start, (blocks, w_gate, w_up, w_down))
    return (total_grad.astype(jnp.bfloat16), total_gate.reshape(TOKENS, TOPK), grads[0], grads[1], grads[2])
```

```python
import jax
import jax.numpy as jnp
from jax import lax
from jax.sharding import PartitionSpec as P


def contract_rows(left, right):
    return lax.dot_general(
        left, right, (((0,), (0,)), ((), ())), preferred_element_type=jnp.float32
    )


def contract_cols(left, right):
    return lax.dot_general(
        left, right, (((1,), (1,)), ((), ())), preferred_element_type=jnp.float32
    )


def expert_math(rows_in, rows_cot, row_gate, w_one, u_one, d_one):
    pre_gate = jnp.dot(rows_in, w_one, preferred_element_type=jnp.float32)
    pre_up = jnp.dot(rows_in, u_one, preferred_element_type=jnp.float32)
    sigma = jax.nn.sigmoid(pre_gate)
    active = pre_gate * sigma
    hidden = (active * pre_up).astype(jnp.bfloat16)
    back_hidden = contract_cols(rows_cot, d_one)
    expert_out = jnp.dot(hidden, d_one, preferred_element_type=jnp.float32)
    gate_term = jnp.sum(rows_cot.astype(jnp.float32) * expert_out, axis=1)
    weight_col = row_gate.astype(jnp.float32)[:, None]
    scaled_back = weight_col * back_hidden
    grad_pre_gate = (scaled_back * pre_up * sigma * (1.0 + pre_gate * (1.0 - sigma))).astype(
        jnp.bfloat16
    )
    grad_pre_up = (scaled_back * active).astype(jnp.bfloat16)
    scaled_hidden = (weight_col * active * pre_up).astype(jnp.bfloat16)
    row_grad = (contract_cols(grad_pre_gate, w_one) + contract_cols(grad_pre_up, u_one)).astype(
        jnp.bfloat16
    )
    return (row_grad, gate_term.astype(jnp.bfloat16), grad_pre_gate, grad_pre_up, scaled_hidden)


def dispatched(tokens, cotangent, expert_ids, gates, w_gate, w_up, w_down):
    token_count = tokens.shape[0]
    model_width = tokens.shape[1]
    top_count = expert_ids.shape[1]
    expert_count = lax.axis_size("expert") * lax.axis_size("dp")
    assigned = token_count * top_count
    slot_count = assigned // expert_count
    position = jnp.arange(assigned, dtype=jnp.int32)
    order = jnp.argsort(expert_ids.reshape(-1) * assigned + position)
    rank = jnp.zeros((assigned,), jnp.int32).at[order].set(position)
    source = order // top_count
    send_in = tokens[source].reshape(expert_count, slot_count, model_width)
    send_cot = cotangent[source].reshape(expert_count, slot_count, model_width)
    send_gate = gates.reshape(-1)[order].reshape(expert_count, slot_count)
    w_one = w_gate[0]
    u_one = w_up[0]
    d_one = w_down[0]
    rows_in = lax.all_to_all(send_in, ("expert", "dp"), split_axis=0, concat_axis=0, tiled=True)
    rows_cot = lax.all_to_all(send_cot, ("expert", "dp"), split_axis=0, concat_axis=0, tiled=True)
    row_gate = lax.all_to_all(send_gate, ("expert", "dp"), split_axis=0, concat_axis=0, tiled=True)
    senders = rows_in.shape[0]
    width_slots = rows_in.shape[1]
    outputs = expert_math(
        rows_in.reshape(-1, model_width),
        rows_cot.reshape(-1, model_width),
        row_gate.reshape(-1),
        w_one,
        u_one,
        d_one,
    )
    back_rows = lax.all_to_all(
        outputs[0].reshape(senders, width_slots, model_width),
        ("expert", "dp"),
        split_axis=0,
        concat_axis=0,
        tiled=True,
    )
    back_gate = lax.all_to_all(
        outputs[1].reshape(senders, width_slots),
        ("expert", "dp"),
        split_axis=0,
        concat_axis=0,
        tiled=True,
    )
    results = (
        back_rows,
        back_gate,
        rows_in,
        rows_cot,
        outputs[2].reshape(senders, width_slots, -1),
        outputs[3].reshape(senders, width_slots, -1),
        outputs[4].reshape(senders, width_slots, -1),
    )
    back_rows, back_gate, recv_in, recv_cot, grad_pre_gate, grad_pre_up, scaled_hidden = results
    recv_in = recv_in.reshape(-1, model_width)
    recv_cot = recv_cot.reshape(-1, model_width)
    grad_pre_gate = grad_pre_gate.reshape(assigned, -1)
    grad_pre_up = grad_pre_up.reshape(assigned, -1)
    scaled_hidden = scaled_hidden.reshape(assigned, -1)
    grad_w_gate = contract_rows(recv_in, grad_pre_gate).astype(jnp.bfloat16)
    grad_w_up = contract_rows(recv_in, grad_pre_up).astype(jnp.bfloat16)
    grad_w_down = contract_rows(scaled_hidden, recv_cot).astype(jnp.bfloat16)
    back_flat = back_rows.reshape(assigned, model_width)[rank]
    tokens_grad = jnp.sum(
        back_flat.reshape(token_count, top_count, model_width).astype(jnp.float32), axis=1
    )
    gates_grad = back_gate.reshape(-1)[rank].reshape(token_count, top_count)
    return (
        tokens_grad.astype(jnp.bfloat16),
        gates_grad,
        grad_w_gate[None],
        grad_w_up[None],
        grad_w_down[None],
    )

CORES = 2


def expert_columns(values, width):
    return jnp.concatenate(
        [jnp.broadcast_to(values[:, i : i + 1], (values.shape[0], width)) for i in range(values.shape[1])], axis=1
    )


def chunk_math(rows_in, rows_cot, gate_cols, w_both, u_both, d_both):
    hidden_units = w_both.shape[1] // CORES
    pre_gate = jnp.dot(rows_in, w_both, preferred_element_type=jnp.float32)
    pre_up = jnp.dot(rows_in, u_both, preferred_element_type=jnp.float32)
    back_hidden = contract_cols(rows_cot, d_both)
    sigma = jax.nn.sigmoid(pre_gate)
    active = pre_gate * sigma
    hidden = (active * pre_up).astype(jnp.bfloat16)
    product = hidden.astype(jnp.float32) * back_hidden
    gate_term = jnp.sum(product.reshape(-1, CORES, hidden_units), axis=2).astype(jnp.bfloat16)
    weight = expert_columns(gate_cols.astype(jnp.float32), hidden_units)
    scaled_back = weight * back_hidden
    grad_pre_gate = (scaled_back * pre_up * sigma * (1.0 + pre_gate * (1.0 - sigma))).astype(jnp.bfloat16)
    grad_pre_up = (scaled_back * active).astype(jnp.bfloat16)
    scaled_hidden = (weight * active * pre_up).astype(jnp.bfloat16)
    row_grad = contract_cols(grad_pre_gate, w_both) + contract_cols(grad_pre_up, u_both)
    return row_grad, gate_term, grad_pre_gate, grad_pre_up, scaled_hidden


def gathered(tokens, cotangent, expert_ids, gates, w_gate, w_up, w_down):
    z_count = lax.axis_size("expert")
    dp_count = lax.axis_size("dp")
    x_count = dp_count // CORES
    expert_count = z_count * dp_count
    token_count = tokens.shape[0]
    z_here = lax.axis_index("expert")
    dp_here = lax.axis_index("dp")

    def z_shift(value, step):
        return lax.ppermute(value, "expert", [(i, (i + step) % z_count) for i in range(z_count)])

    def x_shift(value, step):
        return lax.ppermute(value, "dp", [(i, (i + CORES * step) % dp_count) for i in range(dp_count)])

    def core_swap(value):
        return lax.ppermute(value, "dp", [(i, i ^ 1) for i in range(dp_count)])

    expert_range = jnp.arange(expert_count, dtype=jnp.int32)
    chosen = expert_ids[:, :, None] == expert_range
    gate_table = jnp.sum(jnp.where(chosen, gates[:, :, None].astype(jnp.float32), 0.0), axis=1).astype(jnp.bfloat16)

    w_both = jnp.concatenate([w_gate[0], core_swap(w_gate[0])], axis=1)
    u_both = jnp.concatenate([w_up[0], core_swap(w_up[0])], axis=1)
    d_both = jnp.concatenate([w_down[0], core_swap(w_down[0])], axis=0)

    tables = [gate_table] + [z_shift(gate_table, d) for d in range(1, z_count)]
    table_stack = jnp.stack(tables)
    table_lines = [table_stack] + [x_shift(table_stack, s) for s in range(1, x_count)]
    own_expert = z_here * dp_count + dp_here
    mate_expert = z_here * dp_count + (dp_here ^ 1)
    pick = (expert_range[:, None] == jnp.stack([own_expert, mate_expert])[None, :]).astype(jnp.bfloat16)

    held_in, held_cot = [tokens], [cotangent]
    for d in range(1, z_count):
        held_in.append(z_shift(held_in[-1], 1))
        held_cot.append(z_shift(held_cot[-1], 1))

    rows_in, rows_cot, parts, row_grads = [], [], [], []
    for d in range(z_count):
        block_in = jnp.concatenate([held_in[d]] + [x_shift(held_in[d], s) for s in range(1, x_count)])
        block_cot = jnp.concatenate([held_cot[d]] + [x_shift(held_cot[d], s) for s in range(1, x_count)])
        table = jnp.concatenate([line[d] for line in table_lines])
        gate_cols = jnp.dot(table, pick, preferred_element_type=jnp.float32)
        outs = chunk_math(block_in, block_cot, gate_cols, w_both, u_both, d_both)
        rows_in.append(block_in)
        rows_cot.append(block_cot)
        row_grads.append(outs[0].reshape(x_count, token_count, -1))
        parts.append(outs[1:])

    total = None
    for d in list(range(1, z_count)) + [0]:
        line = row_grads[d][0]
        for s in range(1, x_count):
            line = line + x_shift(row_grads[d][s].astype(jnp.bfloat16), x_count - s).astype(jnp.float32)
        if d:
            line = z_shift(line.astype(jnp.bfloat16), z_count - d).astype(jnp.float32)
        total = line if total is None else total + line
    tokens_grad = total.astype(jnp.bfloat16)

    terms = jnp.stack([p[0].reshape(x_count, token_count, CORES) for p in parts])
    columns = [terms[:, 0]] + [x_shift(terms[:, s], x_count - s) for s in range(1, x_count)]
    columns = jnp.concatenate(columns, axis=2)
    back = [columns[0]] + [z_shift(columns[d], z_count - d) for d in range(1, z_count)]
    back = jnp.concatenate(back, axis=1)
    column_ids = []
    for d in range(z_count):
        for s in range(x_count):
            dp_from = (dp_here + CORES * s) % dp_count
            first = ((z_here + d) % z_count) * dp_count
            column_ids += [first + dp_from, first + (dp_from ^ 1)]
    same = expert_ids[:, :, None] == jnp.stack(column_ids)
    gates_grad = jnp.sum(jnp.where(same, back[:, None, :].astype(jnp.float32), 0.0), axis=2).astype(jnp.bfloat16)

    all_in = jnp.concatenate(rows_in)
    all_cot = jnp.concatenate(rows_cot)
    g_gate = jnp.concatenate([p[1] for p in parts])
    g_up = jnp.concatenate([p[2] for p in parts])
    hid = jnp.concatenate([p[3] for p in parts])
    f = w_gate.shape[2]
    mate = (
        contract_rows(all_in, g_gate[:, f:]).astype(jnp.bfloat16),
        contract_rows(all_in, g_up[:, f:]).astype(jnp.bfloat16),
        contract_rows(hid[:, f:], all_cot).astype(jnp.bfloat16),
    )
    mine = (
        contract_rows(all_in, g_gate[:, :f]),
        contract_rows(all_in, g_up[:, :f]),
        contract_rows(hid[:, :f], all_cot),
    )
    grads = [(a + core_swap(b).astype(jnp.float32)).astype(jnp.bfloat16)[None] for a, b in zip(mine, mate)]
    return (tokens_grad, gates_grad, *grads)


def per_device(tokens, cotangent, expert_ids, gates, w_gate, w_up, w_down):
    expert_count = lax.axis_size("expert") * lax.axis_size("dp")
    plan = gathered if expert_count <= 4 * expert_ids.shape[1] and lax.axis_size("dp") % CORES == 0 else dispatched
    return plan(tokens, cotangent, expert_ids, gates, w_gate, w_up, w_down)


def solution(mesh):
    placed = (
        P(("group", "expert", "dp"), None),
        P(("group", "expert", "dp"), None),
        P(("group", "expert", "dp"), None),
        P(("group", "expert", "dp"), None),
        P(("expert", "dp"), None, None),
        P(("expert", "dp"), None, None),
        P(("expert", "dp"), None, None),
    )
    return jax.shard_map(
        per_device,
        mesh=mesh,
        in_specs=placed,
        out_specs=(
            P(("group", "expert", "dp"), None),
            P(("group", "expert", "dp"), None),
            P(("group", "expert", "dp"), None, None),
            P(("group", "expert", "dp"), None, None),
            P(("group", "expert", "dp"), None, None),
        ),
        check_vma=False,
    )
```

```python
import jax
import jax.numpy as jnp
from jax import lax
from jax.experimental import pallas as pl
from jax.experimental.pallas import tpu as pltpu
from jax.sharding import PartitionSpec as P


def contract_rows(left, right):
    return lax.dot_general(
        left, right, (((0,), (0,)), ((), ())), preferred_element_type=jnp.float32
    )


def contract_cols(left, right):
    return lax.dot_general(
        left, right, (((1,), (1,)), ((), ())), preferred_element_type=jnp.float32
    )


def expert_math(rows_in, rows_cot, row_gate, w_one, u_one, d_one):
    pre_gate = jnp.dot(rows_in, w_one, preferred_element_type=jnp.float32)
    pre_up = jnp.dot(rows_in, u_one, preferred_element_type=jnp.float32)
    sigma = jax.nn.sigmoid(pre_gate)
    active = pre_gate * sigma
    hidden = (active * pre_up).astype(jnp.bfloat16)
    back_hidden = contract_cols(rows_cot, d_one)
    expert_out = jnp.dot(hidden, d_one, preferred_element_type=jnp.float32)
    gate_term = jnp.sum(rows_cot.astype(jnp.float32) * expert_out, axis=1)
    weight_col = row_gate.astype(jnp.float32)[:, None]
    scaled_back = weight_col * back_hidden
    grad_pre_gate = (scaled_back * pre_up * sigma * (1.0 + pre_gate * (1.0 - sigma))).astype(
        jnp.bfloat16
    )
    grad_pre_up = (scaled_back * active).astype(jnp.bfloat16)
    scaled_hidden = (weight_col * active * pre_up).astype(jnp.bfloat16)
    row_grad = (contract_cols(grad_pre_gate, w_one) + contract_cols(grad_pre_up, u_one)).astype(
        jnp.bfloat16
    )
    return (row_grad, gate_term.astype(jnp.bfloat16), grad_pre_gate, grad_pre_up, scaled_hidden)


def dispatched(tokens, cotangent, expert_ids, gates, w_gate, w_up, w_down):
    token_count = tokens.shape[0]
    model_width = tokens.shape[1]
    top_count = expert_ids.shape[1]
    expert_count = lax.axis_size("expert") * lax.axis_size("dp")
    assigned = token_count * top_count
    slot_count = assigned // expert_count
    position = jnp.arange(assigned, dtype=jnp.int32)
    order = jnp.argsort(expert_ids.reshape(-1) * assigned + position)
    rank = jnp.zeros((assigned,), jnp.int32).at[order].set(position)
    source = order // top_count
    send_in = tokens[source].reshape(expert_count, slot_count, model_width)
    send_cot = cotangent[source].reshape(expert_count, slot_count, model_width)
    send_gate = gates.reshape(-1)[order].reshape(expert_count, slot_count)
    w_one = w_gate[0]
    u_one = w_up[0]
    d_one = w_down[0]
    rows_in = lax.all_to_all(send_in, ("expert", "dp"), split_axis=0, concat_axis=0, tiled=True)
    rows_cot = lax.all_to_all(send_cot, ("expert", "dp"), split_axis=0, concat_axis=0, tiled=True)
    row_gate = lax.all_to_all(send_gate, ("expert", "dp"), split_axis=0, concat_axis=0, tiled=True)
    senders = rows_in.shape[0]
    width_slots = rows_in.shape[1]
    outputs = expert_math(
        rows_in.reshape(-1, model_width),
        rows_cot.reshape(-1, model_width),
        row_gate.reshape(-1),
        w_one,
        u_one,
        d_one,
    )
    back_rows = lax.all_to_all(
        outputs[0].reshape(senders, width_slots, model_width),
        ("expert", "dp"),
        split_axis=0,
        concat_axis=0,
        tiled=True,
    )
    back_gate = lax.all_to_all(
        outputs[1].reshape(senders, width_slots),
        ("expert", "dp"),
        split_axis=0,
        concat_axis=0,
        tiled=True,
    )
    results = (
        back_rows,
        back_gate,
        rows_in,
        rows_cot,
        outputs[2].reshape(senders, width_slots, -1),
        outputs[3].reshape(senders, width_slots, -1),
        outputs[4].reshape(senders, width_slots, -1),
    )
    back_rows, back_gate, recv_in, recv_cot, grad_pre_gate, grad_pre_up, scaled_hidden = results
    recv_in = recv_in.reshape(-1, model_width)
    recv_cot = recv_cot.reshape(-1, model_width)
    grad_pre_gate = grad_pre_gate.reshape(assigned, -1)
    grad_pre_up = grad_pre_up.reshape(assigned, -1)
    scaled_hidden = scaled_hidden.reshape(assigned, -1)
    grad_w_gate = contract_rows(recv_in, grad_pre_gate).astype(jnp.bfloat16)
    grad_w_up = contract_rows(recv_in, grad_pre_up).astype(jnp.bfloat16)
    grad_w_down = contract_rows(scaled_hidden, recv_cot).astype(jnp.bfloat16)
    back_flat = back_rows.reshape(assigned, model_width)[rank]
    tokens_grad = jnp.sum(
        back_flat.reshape(token_count, top_count, model_width).astype(jnp.float32), axis=1
    )
    gates_grad = back_gate.reshape(-1)[rank].reshape(token_count, top_count)
    return (
        tokens_grad.astype(jnp.bfloat16),
        gates_grad,
        grad_w_gate[None],
        grad_w_up[None],
        grad_w_down[None],
    )

CORES = 2
TILE = 256
LANES = 128


def wait_for(copies):
    for copy in copies:
        copy.wait()


def tiles(count, body):
    @pl.loop(0, count // TILE)
    def _(i):
        body(pl.ds(pl.multiple_of(i * TILE, TILE), TILE))


def row_tiles(count, size, body):
    @pl.loop(0, count // size)
    def _(i):
        body(pl.ds(pl.multiple_of(i * size, size), size))


def forward_kernel(lines, step, token_count, f, *refs):
    refs = list(refs)
    take = lambda n: [refs.pop(0) for _ in range(n)]
    tok_in, gate_w, up_w = take(lines), take(CORES), take(CORES)
    if step:
        take(1)
    slope_ref, active_ref, product_ref, tok_all = take(4)
    tok, wg, wu, pre_gate, in_sem, out_sem = take(6)
    rows = lines * token_count
    slot = iter(range(64))
    copy_in = lambda src, dst: pltpu.make_async_copy(src, dst, in_sem.at[next(slot)])
    columns = [pl.ds(e * f, f) for e in range(CORES)]
    first = [copy_in(tok_in[i], tok.at[pl.ds(i * token_count, token_count)]) for i in range(lines)]
    first += [copy_in(gate_w[e], wg.at[:, columns[e]]) for e in range(CORES)]
    second = [copy_in(up_w[e], wu.at[:, columns[e]]) for e in range(CORES)]
    for copy in first + second:
        copy.start()
    wait_for(first)
    keep = pltpu.make_async_copy(tok, tok_all.at[pl.ds(step * rows, rows)], out_sem.at[0])
    keep.start()

    def gate_tile(c):
        pre_gate[:, c] = jnp.dot(tok[...], wg[:, c], preferred_element_type=jnp.float32)

    def up_tile(c):
        up = jnp.dot(tok[...], wu[:, c], preferred_element_type=jnp.float32)
        gate = pre_gate[:, c]
        sigma = jax.nn.sigmoid(gate)
        active = gate * sigma
        slope_ref[:, c] = up * sigma * (1.0 + gate * (1.0 - sigma))
        active_ref[:, c] = active
        product_ref[:, c] = active * up

    tiles(CORES * f, gate_tile)
    wait_for(second)
    tiles(CORES * f, up_tile)
    keep.wait()


def backward_kernel(lines, step, token_count, f, *refs):
    refs = list(refs)
    take = lambda n: [refs.pop(0) for _ in range(n)]
    cot_in, (pick_ref,), hidden_in = take(lines), take(1), take(3)
    gate_w, up_w, down_w = take(CORES), take(CORES), take(CORES)
    if step:
        take(7)
    row_own, row_far, terms, cot_all = take(4)
    factor_all = take(6)
    cot, wg, wu, wd, slope, active, product, back, gg, gu = take(10)
    factors = take(6)
    in_sem, out_sem = take(2)
    rows = lines * token_count
    model_width = wd.shape[1]
    slot = iter(range(64))
    copy_in = lambda src, dst: pltpu.make_async_copy(src, dst, in_sem.at[next(slot)])
    columns = [pl.ds(e * f, f) for e in range(CORES)]
    first = [copy_in(cot_in[i], cot.at[pl.ds(i * token_count, token_count)]) for i in range(lines)]
    first += [copy_in(down_w[e], wd.at[columns[e]]) for e in range(CORES)]
    second = [copy_in(a, b) for a, b in zip(hidden_in, (slope, active, product))]
    third = [copy_in(gate_w[e], wg.at[:, columns[e]]) for e in range(CORES)]
    third += [copy_in(up_w[e], wu.at[:, columns[e]]) for e in range(CORES)]
    for copy in first + second + third:
        copy.start()
    wait_for(first)
    at = pl.ds(step * rows, rows)
    keep = pltpu.make_async_copy(cot.at[:, :model_width], cot_all.at[at], out_sem.at[0])
    keep.start()

    def back_tile(c):
        back[:, c] = contract_cols(cot[:, :model_width], wd[c, :])

    def factor_tile(r):
        gate_cols = jnp.dot(cot[r, model_width:], pick_ref[...], preferred_element_type=jnp.float32)
        sums = []
        for e in range(CORES):
            c = columns[e]
            bh, prod = back[r, c], product[r, c]
            hidden = prod.astype(jnp.bfloat16)
            sums.append(jnp.sum(hidden.astype(jnp.float32) * bh, axis=1, keepdims=True))
            weight = gate_cols[:, e : e + 1]
            scaled_back = weight * bh
            grad_gate = (scaled_back * slope[r, c]).astype(jnp.bfloat16)
            grad_up = (scaled_back * active[r, c]).astype(jnp.bfloat16)
            gg[r, c] = grad_gate
            gu[r, c] = grad_up
            factors[e][r, :] = grad_gate
            factors[CORES + e][r, :] = grad_up
            factors[2 * CORES + e][r, :] = (weight * prod).astype(jnp.bfloat16)
        lane = lax.broadcasted_iota(jnp.int32, sums[0].shape[:1] + (CORES,), 1)
        terms[r, :] = jnp.where(lane == 0, sums[0], sums[1])

    def row_tile(c):
        grad = contract_cols(gg[...], wg[c, :]) + contract_cols(gu[...], wu[c, :])
        row_own[:, c] = grad[:token_count]
        row_far[:, c] = grad[token_count:].astype(jnp.bfloat16)

    tiles(CORES * f, back_tile)
    wait_for(second)
    row_tiles(rows, 64, factor_tile)
    out_copies = [
        pltpu.make_async_copy(a, b.at[at], out_sem.at[1 + i]) for i, (a, b) in enumerate(zip(factors, factor_all))
    ]
    for copy in out_copies:
        copy.start()
    wait_for(third)
    tiles(model_width, row_tile)
    wait_for([keep] + out_copies)


HBM = pl.BlockSpec(memory_space=pltpu.HBM)
VMEM = pl.BlockSpec(memory_space=pltpu.VMEM)
PARAMS = pltpu.CompilerParams(vmem_limit_bytes=60 * 1024 * 1024)


def forward(step, steps, blocks, weights, held):
    lines = len(blocks)
    token_count, model_width = blocks[0].shape
    f = weights[0].shape[1]
    rows, wide = lines * token_count, CORES * f
    ins = [*blocks, *weights[: 2 * CORES], *held]
    hidden = jax.ShapeDtypeStruct((rows, wide), jnp.float32)
    outs = pl.pallas_call(
        lambda *refs: forward_kernel(lines, step, token_count, f, *refs),
        out_shape=[hidden] * 3 + [jax.ShapeDtypeStruct((steps * rows, model_width), jnp.bfloat16)],
        in_specs=[HBM] * len(ins),
        out_specs=[VMEM] * 3 + [HBM],
        scratch_shapes=[
            pltpu.VMEM((rows, model_width), jnp.bfloat16),
            pltpu.VMEM((model_width, wide), jnp.bfloat16),
            pltpu.VMEM((model_width, wide), jnp.bfloat16),
            pltpu.VMEM((rows, wide), jnp.float32),
            pltpu.SemaphoreType.DMA((lines + 2 * CORES,)),
            pltpu.SemaphoreType.DMA((1,)),
        ],
        input_output_aliases={len(ins) - 1: 3} if held else {},
        compiler_params=PARAMS,
        cost_estimate=pl.CostEstimate(
            flops=4 * rows * model_width * wide,
            bytes_accessed=4 * model_width * wide + 4 * rows * model_width,
            transcendentals=rows * wide,
        ),
    )(*ins)
    return list(outs[:3]), [outs[3]]


def backward(step, steps, blocks, pick, hidden, weights, held):
    lines = len(blocks)
    token_count, padded = blocks[0].shape
    model_width, f = weights[0].shape
    rows, wide = lines * token_count, CORES * f
    bf = jnp.bfloat16
    ins = [*blocks, pick, *hidden, *weights, *held]
    whole = [jax.ShapeDtypeStruct((steps * rows, model_width), bf)]
    whole += [jax.ShapeDtypeStruct((steps * rows, f), bf)] * 6
    out_shape = [
        jax.ShapeDtypeStruct((token_count, model_width), jnp.float32),
        jax.ShapeDtypeStruct(((lines - 1) * token_count, model_width), bf),
        jax.ShapeDtypeStruct((rows, CORES), jnp.float32),
        *whole,
    ]
    base = len(ins) - len(held)
    scratch = [pltpu.VMEM((rows, padded), bf)]
    scratch += [pltpu.VMEM((model_width, wide), bf)] * 2 + [pltpu.VMEM((wide, model_width), bf)]
    scratch += [pltpu.VMEM((rows, wide), jnp.float32)] * 4 + [pltpu.VMEM((rows, wide), bf)] * 2
    scratch += [pltpu.VMEM((rows, f), bf)] * 6
    scratch += [pltpu.SemaphoreType.DMA((lines + 3 + 3 * CORES,)), pltpu.SemaphoreType.DMA((7,))]
    outs = pl.pallas_call(
        lambda *refs: backward_kernel(lines, step, token_count, f, *refs),
        out_shape=out_shape,
        in_specs=[HBM] * lines + [VMEM] + [HBM] * (len(ins) - lines - 1),
        out_specs=[VMEM] * 3 + [HBM] * len(whole),
        scratch_shapes=scratch,
        input_output_aliases={base + i: 3 + i for i in range(len(held))},
        compiler_params=PARAMS,
        cost_estimate=pl.CostEstimate(
            flops=6 * rows * model_width * wide,
            bytes_accessed=6 * model_width * wide + 8 * rows * model_width,
            transcendentals=0,
        ),
    )(*ins)
    return outs[0], outs[1], outs[2], list(outs[3:])


def gathered(tokens, cotangent, expert_ids, gates, w_gate, w_up, w_down):
    z_count = lax.axis_size("expert")
    dp_count = lax.axis_size("dp")
    x_count = dp_count // CORES
    expert_count = z_count * dp_count
    token_count = tokens.shape[0]
    z_here = lax.axis_index("expert")
    dp_here = lax.axis_index("dp")

    def z_shift(value, step):
        return lax.ppermute(value, "expert", [(i, (i + step) % z_count) for i in range(z_count)])

    def x_shift(value, step):
        return lax.ppermute(value, "dp", [(i, (i + CORES * step) % dp_count) for i in range(dp_count)])

    def core_swap(value):
        return lax.ppermute(value, "dp", [(i, i ^ 1) for i in range(dp_count)])

    expert_range = jnp.arange(expert_count, dtype=jnp.int32)
    chosen = expert_ids[:, :, None] == expert_range
    gate_table = jnp.sum(jnp.where(chosen, gates[:, :, None].astype(jnp.float32), 0.0), axis=1).astype(jnp.bfloat16)

    table_width = -(-expert_count // LANES) * LANES
    gate_table = jnp.pad(gate_table, ((0, 0), (0, table_width - expert_count)))
    cot_gates = jnp.concatenate([cotangent, gate_table], axis=1)
    own_expert = z_here * dp_count + dp_here
    mate_expert = z_here * dp_count + (dp_here ^ 1)
    pick_row = jnp.arange(table_width, dtype=jnp.int32)[:, None]
    pick_column = jnp.arange(LANES, dtype=jnp.int32)[None, :]
    wanted = jnp.where(pick_column == 0, own_expert, mate_expert)
    pick = ((pick_row == wanted) & (pick_column < CORES)).astype(jnp.bfloat16)

    def after(value, *earlier):
        return lax.optimization_barrier((value, *earlier))[0]

    def across(block):
        return [block] + [x_shift(block, s) for s in range(1, x_count)]

    def home(d):
        line = row_own[d]
        for s in range(1, x_count):
            line = line + x_shift(row_far[d][s - 1], x_count - s).astype(jnp.float32)
        return line.astype(jnp.bfloat16) if d else line

    blocks_in, blocks_cot = [across(tokens)], [across(cot_gates)]
    ring_in, ring_cot = z_shift(tokens, 1), z_shift(cot_gates, 1)
    weights = []
    for own in (w_gate[0], w_up[0], w_down[0]):
        weights += [own, core_swap(after(own, *weights[-1:]))]

    row_own, row_far, terms, lines, rows_held, held = [], [], [], [None] * z_count, [], []
    for d in range(z_count):
        more = d + 1 < z_count
        if more:
            blocks_in.append(across(ring_in))
            next_in = z_shift(ring_in, 1) if d + 2 < z_count else None
            ready = ring_in
        elif z_count > 2:
            ready = lines[1] = home(1)
        else:
            ready = pick
        blocks_in[d][0] = after(blocks_in[d][0], ready)
        hidden, rows_held = forward(d, z_count, blocks_in[d], weights, rows_held)
        if more:
            ring_cot = after(ring_cot, hidden[0])
            blocks_cot.append(across(ring_cot))
            next_cot = z_shift(ring_cot, 1) if d + 2 < z_count else None
            ready = ring_cot
        own, far, term, held = backward(d, z_count, blocks_cot[d], after(pick, ready), hidden, weights, held)
        if d + 2 < z_count:
            ring_in, ring_cot = after(next_in, term), next_cot
        row_own.append(own)
        row_far.append(far.reshape(x_count - 1, token_count, -1))
        terms.append(term)
    for d in range(2, z_count - 1):
        row_own[d] = after(row_own[d], terms[-1])

    row_far[0], row_far[-1] = lax.optimization_barrier((row_far[0], row_far[-1]))
    total = None
    for d in list(range(1, z_count)) + [0]:
        line = home(d) if lines[d] is None else lines[d]
        if d:
            line = z_shift(line, z_count - d).astype(jnp.float32)
        total = line if total is None else total + line
    tokens_grad = total.astype(jnp.bfloat16)

    terms = jnp.stack(terms).astype(jnp.bfloat16).reshape(z_count, x_count, token_count, CORES)
    columns = [terms[:, 0]] + [x_shift(terms[:, s], x_count - s) for s in range(1, x_count)]
    columns = jnp.concatenate(columns, axis=2)
    back = [columns[0]] + [z_shift(columns[d], z_count - d) for d in range(1, z_count)]
    back = jnp.concatenate(back, axis=1)
    column_ids = []
    for d in range(z_count):
        for s in range(x_count):
            dp_from = (dp_here + CORES * s) % dp_count
            first = ((z_here + d) % z_count) * dp_count
            column_ids += [first + dp_from, first + (dp_from ^ 1)]
    same = expert_ids[:, :, None] == jnp.stack(column_ids)
    gates_grad = jnp.sum(jnp.where(same, back[:, None, :].astype(jnp.float32), 0.0), axis=2).astype(jnp.bfloat16)

    all_in, all_cot = rows_held[0], held[0]
    gate_own, gate_mate, up_own, up_mate, hid_own, hid_mate = held[1:]
    mate = (
        contract_rows(all_in, gate_mate).astype(jnp.bfloat16),
        contract_rows(all_in, up_mate).astype(jnp.bfloat16),
        contract_rows(hid_mate, all_cot).astype(jnp.bfloat16),
    )
    mine = (
        contract_rows(all_in, gate_own),
        contract_rows(all_in, up_own),
        contract_rows(hid_own, all_cot),
    )
    grads = [(a + core_swap(b).astype(jnp.float32)).astype(jnp.bfloat16)[None] for a, b in zip(mine, mate)]
    return (tokens_grad, gates_grad, *grads)


def per_device(tokens, cotangent, expert_ids, gates, w_gate, w_up, w_down):
    expert_count = lax.axis_size("expert") * lax.axis_size("dp")
    plan = gathered if expert_count <= 4 * expert_ids.shape[1] and lax.axis_size("dp") % CORES == 0 else dispatched
    return plan(tokens, cotangent, expert_ids, gates, w_gate, w_up, w_down)


def solution(mesh):
    placed = (
        P(("group", "expert", "dp"), None),
        P(("group", "expert", "dp"), None),
        P(("group", "expert", "dp"), None),
        P(("group", "expert", "dp"), None),
        P(("expert", "dp"), None, None),
        P(("expert", "dp"), None, None),
        P(("expert", "dp"), None, None),
    )
    return jax.shard_map(
        per_device,
        mesh=mesh,
        in_specs=placed,
        out_specs=(
            P(("group", "expert", "dp"), None),
            P(("group", "expert", "dp"), None),
            P(("group", "expert", "dp"), None, None),
            P(("group", "expert", "dp"), None, None),
            P(("group", "expert", "dp"), None, None),
        ),
        check_vma=False,
    )
```

```python
import jax
import jax.numpy as jnp
from jax import lax
from jax.experimental import pallas as pl
from jax.experimental.pallas import tpu as pltpu
from jax.sharding import PartitionSpec as P


def contract_rows(left, right):
    return lax.dot_general(
        left, right, (((0,), (0,)), ((), ())), preferred_element_type=jnp.float32
    )


def contract_cols(left, right):
    return lax.dot_general(
        left, right, (((1,), (1,)), ((), ())), preferred_element_type=jnp.float32
    )


def expert_math(rows_in, rows_cot, row_gate, w_one, u_one, d_one):
    pre_gate = jnp.dot(rows_in, w_one, preferred_element_type=jnp.float32)
    pre_up = jnp.dot(rows_in, u_one, preferred_element_type=jnp.float32)
    sigma = jax.nn.sigmoid(pre_gate)
    active = pre_gate * sigma
    hidden = (active * pre_up).astype(jnp.bfloat16)
    back_hidden = contract_cols(rows_cot, d_one)
    expert_out = jnp.dot(hidden, d_one, preferred_element_type=jnp.float32)
    gate_term = jnp.sum(rows_cot.astype(jnp.float32) * expert_out, axis=1)
    weight_col = row_gate.astype(jnp.float32)[:, None]
    scaled_back = weight_col * back_hidden
    grad_pre_gate = (scaled_back * pre_up * sigma * (1.0 + pre_gate * (1.0 - sigma))).astype(
        jnp.bfloat16
    )
    grad_pre_up = (scaled_back * active).astype(jnp.bfloat16)
    scaled_hidden = (weight_col * active * pre_up).astype(jnp.bfloat16)
    row_grad = (contract_cols(grad_pre_gate, w_one) + contract_cols(grad_pre_up, u_one)).astype(
        jnp.bfloat16
    )
    return (row_grad, gate_term.astype(jnp.bfloat16), grad_pre_gate, grad_pre_up, scaled_hidden)


def dispatched(tokens, cotangent, expert_ids, gates, w_gate, w_up, w_down):
    token_count = tokens.shape[0]
    model_width = tokens.shape[1]
    top_count = expert_ids.shape[1]
    expert_count = lax.axis_size("expert") * lax.axis_size("dp")
    assigned = token_count * top_count
    slot_count = assigned // expert_count
    position = jnp.arange(assigned, dtype=jnp.int32)
    order = jnp.argsort(expert_ids.reshape(-1) * assigned + position)
    rank = jnp.zeros((assigned,), jnp.int32).at[order].set(position)
    source = order // top_count
    send_in = tokens[source].reshape(expert_count, slot_count, model_width)
    send_cot = cotangent[source].reshape(expert_count, slot_count, model_width)
    send_gate = gates.reshape(-1)[order].reshape(expert_count, slot_count)
    w_one = w_gate[0]
    u_one = w_up[0]
    d_one = w_down[0]
    rows_in = lax.all_to_all(send_in, ("expert", "dp"), split_axis=0, concat_axis=0, tiled=True)
    rows_cot = lax.all_to_all(send_cot, ("expert", "dp"), split_axis=0, concat_axis=0, tiled=True)
    row_gate = lax.all_to_all(send_gate, ("expert", "dp"), split_axis=0, concat_axis=0, tiled=True)
    senders = rows_in.shape[0]
    width_slots = rows_in.shape[1]
    outputs = expert_math(
        rows_in.reshape(-1, model_width),
        rows_cot.reshape(-1, model_width),
        row_gate.reshape(-1),
        w_one,
        u_one,
        d_one,
    )
    back_rows = lax.all_to_all(
        outputs[0].reshape(senders, width_slots, model_width),
        ("expert", "dp"),
        split_axis=0,
        concat_axis=0,
        tiled=True,
    )
    back_gate = lax.all_to_all(
        outputs[1].reshape(senders, width_slots),
        ("expert", "dp"),
        split_axis=0,
        concat_axis=0,
        tiled=True,
    )
    results = (
        back_rows,
        back_gate,
        rows_in,
        rows_cot,
        outputs[2].reshape(senders, width_slots, -1),
        outputs[3].reshape(senders, width_slots, -1),
        outputs[4].reshape(senders, width_slots, -1),
    )
    back_rows, back_gate, recv_in, recv_cot, grad_pre_gate, grad_pre_up, scaled_hidden = results
    recv_in = recv_in.reshape(-1, model_width)
    recv_cot = recv_cot.reshape(-1, model_width)
    grad_pre_gate = grad_pre_gate.reshape(assigned, -1)
    grad_pre_up = grad_pre_up.reshape(assigned, -1)
    scaled_hidden = scaled_hidden.reshape(assigned, -1)
    grad_w_gate = contract_rows(recv_in, grad_pre_gate).astype(jnp.bfloat16)
    grad_w_up = contract_rows(recv_in, grad_pre_up).astype(jnp.bfloat16)
    grad_w_down = contract_rows(scaled_hidden, recv_cot).astype(jnp.bfloat16)
    back_flat = back_rows.reshape(assigned, model_width)[rank]
    tokens_grad = jnp.sum(
        back_flat.reshape(token_count, top_count, model_width).astype(jnp.float32), axis=1
    )
    gates_grad = back_gate.reshape(-1)[rank].reshape(token_count, top_count)
    return (
        tokens_grad.astype(jnp.bfloat16),
        gates_grad,
        grad_w_gate[None],
        grad_w_up[None],
        grad_w_down[None],
    )

CORES = 2
ROW_TILE = 1024
FACTOR_ROWS = 128
PRODUCT_TILE = 1024
LANES = 128
HBM = pl.BlockSpec(memory_space=pltpu.HBM)
VMEM = pl.BlockSpec(memory_space=pltpu.VMEM)


def wait_for(copies):
    for copy in copies:
        copy.wait()


def tiles(count, size, body):
    @pl.loop(0, count // size)
    def _(i):
        body(pl.ds(pl.multiple_of(i * size, size), size))


def small_cost(rows, width):
    return pl.CostEstimate(flops=rows * width, bytes_accessed=rows * width, transcendentals=0)


def step_kernel(lines, step, token_count, model_width, f, *refs):
    refs = list(refs)
    take = lambda n: [refs.pop(0) for _ in range(n)]
    blocks, (pick_ref,) = take(lines), take(1)
    gate_w, up_w, down_w = take(CORES), take(CORES), take(CORES)
    if step:
        take(8)
    row_own, row_far = take(2)
    tok_all, cot_all = take(2)
    factor_all = take(6)
    tok, cot, wg, wu, wd, pre_gate, pre_up, back, gg, gu = take(10)
    factors = take(6)
    in_sem, out_sem = take(2)
    rows = lines * token_count
    room = row_own.shape[1] - model_width

    slot = iter(range(64))
    copy_in = lambda src, dst: pltpu.make_async_copy(src, dst, in_sem.at[next(slot)])
    line_rows = [pl.ds(i * token_count, token_count) for i in range(lines)]
    columns = [pl.ds(e * f, f) for e in range(CORES)]
    padded = blocks[0].shape[1] - model_width
    first = [copy_in(blocks[i].at[:, pl.ds(0, model_width)], tok.at[line_rows[i]]) for i in range(lines)]
    first += [copy_in(gate_w[e], wg.at[:, columns[e]]) for e in range(CORES)]
    second = [copy_in(up_w[e], wu.at[:, columns[e]]) for e in range(CORES)]
    third = [copy_in(blocks[i].at[:, pl.ds(model_width, padded)], cot.at[line_rows[i]]) for i in range(lines)]
    third += [copy_in(down_w[e], wd.at[columns[e]]) for e in range(CORES)]
    for copy in first + second + third:
        copy.start()

    def gate_tile(c):
        pre_gate[:, c] = jnp.dot(tok[...], wg[:, c], preferred_element_type=jnp.float32)

    def up_tile(c):
        pre_up[:, c] = jnp.dot(tok[...], wu[:, c], preferred_element_type=jnp.float32)

    def back_tile(c):
        back[:, c] = contract_cols(cot[:, :model_width], wd[c, :])

    def factor_tile(line, r):
        gate_cols = jnp.dot(cot[r, model_width:], pick_ref[...], preferred_element_type=jnp.float32)
        sums = []
        for e in range(CORES):
            c = columns[e]
            gate, up, bh = pre_gate[r, c], pre_up[r, c], back[r, c]
            sigma = jax.nn.sigmoid(gate)
            active = gate * sigma
            prod = active * up
            hidden = prod.astype(jnp.bfloat16)
            sums.append(jnp.sum(hidden.astype(jnp.float32) * bh, axis=1, keepdims=True))
            weight = gate_cols[:, e : e + 1]
            scaled_back = weight * bh
            grad_gate = (scaled_back * up * sigma * (1.0 + gate * (1.0 - sigma))).astype(jnp.bfloat16)
            grad_up = (scaled_back * active).astype(jnp.bfloat16)
            gg[r, c] = grad_gate
            gu[r, c] = grad_up
            factors[e][r, :] = grad_gate
            factors[CORES + e][r, :] = grad_up
            factors[2 * CORES + e][r, :] = (weight * prod).astype(jnp.bfloat16)
        lane = lax.broadcasted_iota(jnp.int32, (sums[0].shape[0], room), 1)
        place = CORES * (step * lines + line)
        found = jnp.where(lane == place, sums[0], jnp.where(lane == place + 1, sums[1], 0.0))
        return found

    def own_terms(r):
        row_own[r, model_width:] = factor_tile(0, r)

    wait_for(first)
    tiles(CORES * f, CORES * f, gate_tile)
    wait_for(second)
    tiles(CORES * f, CORES * f, up_tile)
    wait_for(third)
    tiles(CORES * f, CORES * f, back_tile)
    tiles(token_count, FACTOR_ROWS, own_terms)
    for i in range(1, lines):

        @pl.loop(0, token_count // FACTOR_ROWS)
        def _(j):
            near = pl.ds(pl.multiple_of((i - 1) * token_count + j * FACTOR_ROWS, FACTOR_ROWS), FACTOR_ROWS)
            r = pl.ds(pl.multiple_of(i * token_count + j * FACTOR_ROWS, FACTOR_ROWS), FACTOR_ROWS)
            row_far[near, model_width:] = factor_tile(i, r).astype(jnp.bfloat16)

    at = pl.ds(step * rows, rows)
    outs = [(tok, tok_all), (cot.at[:, pl.ds(0, model_width)], cot_all)] + list(zip(factors, factor_all))
    out_copies = [pltpu.make_async_copy(a, b.at[at], out_sem.at[i]) for i, (a, b) in enumerate(outs)]
    for copy in out_copies:
        copy.start()

    def row_tile(c):
        grad = contract_cols(gg[...], wg[c, :]) + contract_cols(gu[...], wu[c, :])
        row_own[:, c] = grad[:token_count]
        row_far[:, c] = grad[token_count:].astype(jnp.bfloat16)

    tiles(model_width, ROW_TILE, row_tile)
    wait_for(out_copies)


def one_step(step, steps, blocks, pick, weights, held):
    lines = len(blocks)
    token_count = blocks[0].shape[0]
    model_width, f = weights[0].shape
    padded = blocks[0].shape[1] - model_width
    rows, wide = lines * token_count, CORES * f
    bf = jnp.bfloat16
    ins = [*blocks, pick, *weights, *held]
    whole = [jax.ShapeDtypeStruct((steps * rows, model_width), bf)] * 2
    whole += [jax.ShapeDtypeStruct((steps * rows, f), bf)] * 6
    out_shape = [
        jax.ShapeDtypeStruct((token_count, padded), jnp.float32),
        jax.ShapeDtypeStruct(((lines - 1) * token_count, padded), bf),
        *whole,
    ]
    base = len(ins) - len(held)
    scratch = [pltpu.VMEM((rows, model_width), bf), pltpu.VMEM((rows, padded), bf)]
    scratch += [pltpu.VMEM((model_width, wide), bf)] * 2 + [pltpu.VMEM((wide, model_width), bf)]
    scratch += [pltpu.VMEM((rows, wide), jnp.float32)] * 3 + [pltpu.VMEM((rows, wide), bf)] * 2
    scratch += [pltpu.VMEM((rows, f), bf)] * 6
    scratch += [pltpu.SemaphoreType.DMA((2 * lines + 3 * CORES,)), pltpu.SemaphoreType.DMA((8,))]
    outs = pl.pallas_call(
        lambda *refs: step_kernel(lines, step, token_count, model_width, f, *refs),
        out_shape=out_shape,
        in_specs=[HBM] * lines + [VMEM] + [HBM] * (len(ins) - lines - 1),
        out_specs=[VMEM] * 2 + [HBM] * len(whole),
        scratch_shapes=scratch,
        input_output_aliases={base + i: 2 + i for i in range(len(held))},
        compiler_params=pltpu.CompilerParams(vmem_limit_bytes=60 * 1024 * 1024),
        cost_estimate=small_cost(rows, wide),
    )(*ins)
    return outs[0], outs[1], list(outs[2:])


def products_kernel(last, *refs):
    refs = list(refs)
    take = lambda n: [refs.pop(0) for _ in range(n)]
    tok_ref, cot_ref, gate_ref, up_ref, hid_ref = take(5)
    (got_ref,) = take(1) if last else [None]
    outs = take(3) if last else take(1)
    tok, cot, pair, hid = take(4)
    got = take(1)[0] if last else None
    (sem,) = take(1)
    f = hid.shape[1]
    model_width = tok.shape[1]
    slot = iter(range(16))
    copy_in = lambda src, dst: pltpu.make_async_copy(src, dst, sem.at[next(slot)])
    first = [copy_in(gate_ref, pair.at[:, pl.ds(0, f)]), copy_in(up_ref, pair.at[:, pl.ds(f, f)]), copy_in(tok_ref, tok)]
    second = [copy_in(hid_ref, hid), copy_in(cot_ref, cot)]
    if last:
        first.append(copy_in(got_ref, got))
    for copy in first + second:
        copy.start()
    wait_for(first)

    def pair_tile(c):
        both = contract_rows(pair[...], tok[:, c])
        if last:
            both = (both + got[: 2 * f, c].astype(jnp.float32)).astype(jnp.bfloat16).T
            outs[0][c, :] = both[:, :f]
            outs[1][c, :] = both[:, f:]
        else:
            outs[0][: 2 * f, c] = both.astype(jnp.bfloat16)

    def down_tile(c):
        down = contract_rows(hid[...], cot[:, c])
        if last:
            outs[2][:, c] = (down + got[2 * f :, c].astype(jnp.float32)).astype(jnp.bfloat16)
        else:
            outs[0][2 * f :, c] = down.astype(jnp.bfloat16)

    tiles(model_width, PRODUCT_TILE, pair_tile)
    wait_for(second)
    tiles(model_width, PRODUCT_TILE, down_tile)


def products(tok, cot, gate, up, hid, got=None):
    rows, model_width = tok.shape
    f = gate.shape[1]
    bf = jnp.bfloat16
    last = got is not None
    ins = [tok, cot, gate, up, hid] + ([got] if last else [])
    if last:
        out_shape = [jax.ShapeDtypeStruct((model_width, f), bf)] * 2 + [jax.ShapeDtypeStruct((f, model_width), bf)]
    else:
        out_shape = [jax.ShapeDtypeStruct((3 * f, model_width), bf)]
    scratch = [pltpu.VMEM((rows, model_width), bf)] * 2 + [pltpu.VMEM((rows, 2 * f), bf), pltpu.VMEM((rows, f), bf)]
    if last:
        scratch.append(pltpu.VMEM((3 * f, model_width), bf))
    scratch.append(pltpu.SemaphoreType.DMA((7,)))
    return pl.pallas_call(
        lambda *refs: products_kernel(last, *refs),
        out_shape=out_shape,
        in_specs=[HBM] * len(ins),
        out_specs=[VMEM] * len(out_shape),
        scratch_shapes=scratch,
        compiler_params=pltpu.CompilerParams(vmem_limit_bytes=60 * 1024 * 1024),
        cost_estimate=small_cost(rows, 2 * f),
    )(*ins)


def gathered(tokens, cotangent, expert_ids, gates, w_gate, w_up, w_down):
    z_count = lax.axis_size("expert")
    dp_count = lax.axis_size("dp")
    x_count = dp_count // CORES
    expert_count = z_count * dp_count
    token_count, model_width = tokens.shape
    z_here = lax.axis_index("expert")
    dp_here = lax.axis_index("dp")

    def z_shift(value, step):
        return lax.ppermute(value, "expert", [(i, (i + step) % z_count) for i in range(z_count)])

    def x_shift(value, step):
        return lax.ppermute(value, "dp", [(i, (i + CORES * step) % dp_count) for i in range(dp_count)])

    def core_swap(value):
        return lax.ppermute(value, "dp", [(i, i ^ 1) for i in range(dp_count)])

    def after(value, *earlier):
        return lax.optimization_barrier((value, *earlier))[0]

    def across(block):
        return [block] + [x_shift(block, s) for s in range(1, x_count)]

    def home(d, carried=None):
        line = row_own[d]
        for s in range(1, x_count):
            line = line + x_shift(row_far[d][s - 1], x_count - s).astype(jnp.float32)
        if carried is not None:
            line = line + carried.astype(jnp.float32)
        return line.astype(jnp.bfloat16) if d else line

    expert_range = jnp.arange(expert_count, dtype=jnp.int32)
    chosen = expert_ids[:, :, None] == expert_range
    gate_table = jnp.sum(jnp.where(chosen, gates[:, :, None].astype(jnp.float32), 0.0), axis=1).astype(jnp.bfloat16)
    table_width = -(-expert_count // LANES) * LANES
    gate_table = jnp.pad(gate_table, ((0, 0), (0, table_width - expert_count)))
    block = jnp.concatenate([tokens, cotangent, gate_table], axis=1)
    own_expert = z_here * dp_count + dp_here
    mate_expert = z_here * dp_count + (dp_here ^ 1)
    pick_row = jnp.arange(table_width, dtype=jnp.int32)[:, None]
    pick_column = jnp.arange(LANES, dtype=jnp.int32)[None, :]
    wanted = jnp.where(pick_column == 0, own_expert, mate_expert)
    pick = ((pick_row == wanted) & (pick_column < CORES)).astype(jnp.bfloat16)

    weights = []
    for own in (w_gate[0], w_up[0], w_down[0]):
        weights += [own, core_swap(own)]
    ring = z_shift(block, 1)
    pairs = [across(block)]
    ring = after(ring, *weights[1::2])

    row_own, row_far, held, carried = [], [], [], None
    for d in range(z_count):
        ready = []
        if d + 1 < z_count:
            pairs.append(across(ring))
            following = z_shift(ring, 1) if d + 2 < z_count else None
            ready = [ring]
        elif z_count > 2:
            row_own[1] = after(row_own[1], row_far[d - 1])
            carried = home(1)
            ready = [carried]
        own, far, held = one_step(d, z_count, pairs[d], after(pick, *ready), weights, held)
        if d + 1 < z_count:
            far = after(far, pairs[d + 1][-1])
        if d + 2 < z_count:
            ring = after(following, far)
        row_own.append(own)
        row_far.append(far.reshape(x_count - 1, token_count, -1))

    tok_all, cot_all, gate_own, gate_mate, up_own, up_mate, hid_own, hid_mate = held
    row_far[0] = after(row_far[0], row_far[-1])
    for d in range(2, z_count - 1):
        row_own[d] = after(row_own[d], row_own[-1])
        carried = home(d, z_shift(carried, 1))
    if carried is not None:
        hid_mate = after(hid_mate, carried)
    mate = products(tok_all, cot_all, gate_mate, up_mate, hid_mate)[0]
    got = core_swap(mate)
    if z_count > 1:
        row_own[-1] = after(row_own[-1], mate)
        carried = home(z_count - 1, z_shift(carried, 1) if carried is not None else None)
        got = after(got, carried)
        carried = z_shift(carried, 1)
    grads = products(tok_all, cot_all, gate_own, up_own, hid_own, got)

    row_own[0] = after(row_own[0], grads[0])
    total = home(0, carried)
    tokens_grad = total[:, :model_width].astype(jnp.bfloat16)
    back = total[:, model_width : model_width + expert_count]
    column_ids = []
    for d in range(z_count):
        for s in range(x_count):
            dp_from = (dp_here + CORES * s) % dp_count
            first = ((z_here + d) % z_count) * dp_count
            column_ids += [first + dp_from, first + (dp_from ^ 1)]
    same = expert_ids[:, :, None] == jnp.stack(column_ids)
    gates_grad = jnp.sum(jnp.where(same, back[:, None, :], 0.0), axis=2).astype(jnp.bfloat16)
    return (tokens_grad, gates_grad, *[g[None] for g in grads])


def per_device(tokens, cotangent, expert_ids, gates, w_gate, w_up, w_down):
    expert_count = lax.axis_size("expert") * lax.axis_size("dp")
    plan = gathered if expert_count <= 4 * expert_ids.shape[1] and lax.axis_size("dp") % CORES == 0 else dispatched
    return plan(tokens, cotangent, expert_ids, gates, w_gate, w_up, w_down)


def solution(mesh):
    placed = (
        P(("group", "expert", "dp"), None),
        P(("group", "expert", "dp"), None),
        P(("group", "expert", "dp"), None),
        P(("group", "expert", "dp"), None),
        P(("expert", "dp"), None, None),
        P(("expert", "dp"), None, None),
        P(("expert", "dp"), None, None),
    )
    return jax.shard_map(
        per_device,
        mesh=mesh,
        in_specs=placed,
        out_specs=(
            P(("group", "expert", "dp"), None),
            P(("group", "expert", "dp"), None),
            P(("group", "expert", "dp"), None, None),
            P(("group", "expert", "dp"), None, None),
            P(("group", "expert", "dp"), None, None),
        ),
        check_vma=False,
    )
```

```python
import jax
import jax.numpy as jnp
from jax import lax
from jax.experimental import pallas as pl
from jax.experimental.pallas import tpu as pltpu
from jax.sharding import PartitionSpec as P


def contract_rows(left, right):
    return lax.dot_general(
        left, right, (((0,), (0,)), ((), ())), preferred_element_type=jnp.float32
    )


def contract_cols(left, right):
    return lax.dot_general(
        left, right, (((1,), (1,)), ((), ())), preferred_element_type=jnp.float32
    )


def expert_math(rows_in, rows_cot, row_gate, w_one, u_one, d_one):
    pre_gate = jnp.dot(rows_in, w_one, preferred_element_type=jnp.float32)
    pre_up = jnp.dot(rows_in, u_one, preferred_element_type=jnp.float32)
    sigma = jax.nn.sigmoid(pre_gate)
    active = pre_gate * sigma
    hidden = (active * pre_up).astype(jnp.bfloat16)
    back_hidden = contract_cols(rows_cot, d_one)
    expert_out = jnp.dot(hidden, d_one, preferred_element_type=jnp.float32)
    gate_term = jnp.sum(rows_cot.astype(jnp.float32) * expert_out, axis=1)
    weight_col = row_gate.astype(jnp.float32)[:, None]
    scaled_back = weight_col * back_hidden
    grad_pre_gate = (scaled_back * pre_up * sigma * (1.0 + pre_gate * (1.0 - sigma))).astype(
        jnp.bfloat16
    )
    grad_pre_up = (scaled_back * active).astype(jnp.bfloat16)
    scaled_hidden = (weight_col * active * pre_up).astype(jnp.bfloat16)
    row_grad = (contract_cols(grad_pre_gate, w_one) + contract_cols(grad_pre_up, u_one)).astype(
        jnp.bfloat16
    )
    return (row_grad, gate_term.astype(jnp.bfloat16), grad_pre_gate, grad_pre_up, scaled_hidden)


def dispatched(tokens, cotangent, expert_ids, gates, w_gate, w_up, w_down):
    token_count = tokens.shape[0]
    model_width = tokens.shape[1]
    top_count = expert_ids.shape[1]
    expert_count = lax.axis_size("expert") * lax.axis_size("dp")
    assigned = token_count * top_count
    slot_count = assigned // expert_count
    position = jnp.arange(assigned, dtype=jnp.int32)
    order = jnp.argsort(expert_ids.reshape(-1) * assigned + position)
    rank = jnp.zeros((assigned,), jnp.int32).at[order].set(position)
    source = order // top_count
    send_in = tokens[source].reshape(expert_count, slot_count, model_width)
    send_cot = cotangent[source].reshape(expert_count, slot_count, model_width)
    send_gate = gates.reshape(-1)[order].reshape(expert_count, slot_count)
    w_one = w_gate[0]
    u_one = w_up[0]
    d_one = w_down[0]
    rows_in = lax.all_to_all(send_in, ("expert", "dp"), split_axis=0, concat_axis=0, tiled=True)
    rows_cot = lax.all_to_all(send_cot, ("expert", "dp"), split_axis=0, concat_axis=0, tiled=True)
    row_gate = lax.all_to_all(send_gate, ("expert", "dp"), split_axis=0, concat_axis=0, tiled=True)
    senders = rows_in.shape[0]
    width_slots = rows_in.shape[1]
    outputs = expert_math(
        rows_in.reshape(-1, model_width),
        rows_cot.reshape(-1, model_width),
        row_gate.reshape(-1),
        w_one,
        u_one,
        d_one,
    )
    back_rows = lax.all_to_all(
        outputs[0].reshape(senders, width_slots, model_width),
        ("expert", "dp"),
        split_axis=0,
        concat_axis=0,
        tiled=True,
    )
    back_gate = lax.all_to_all(
        outputs[1].reshape(senders, width_slots),
        ("expert", "dp"),
        split_axis=0,
        concat_axis=0,
        tiled=True,
    )
    results = (
        back_rows,
        back_gate,
        rows_in,
        rows_cot,
        outputs[2].reshape(senders, width_slots, -1),
        outputs[3].reshape(senders, width_slots, -1),
        outputs[4].reshape(senders, width_slots, -1),
    )
    back_rows, back_gate, recv_in, recv_cot, grad_pre_gate, grad_pre_up, scaled_hidden = results
    recv_in = recv_in.reshape(-1, model_width)
    recv_cot = recv_cot.reshape(-1, model_width)
    grad_pre_gate = grad_pre_gate.reshape(assigned, -1)
    grad_pre_up = grad_pre_up.reshape(assigned, -1)
    scaled_hidden = scaled_hidden.reshape(assigned, -1)
    grad_w_gate = contract_rows(recv_in, grad_pre_gate).astype(jnp.bfloat16)
    grad_w_up = contract_rows(recv_in, grad_pre_up).astype(jnp.bfloat16)
    grad_w_down = contract_rows(scaled_hidden, recv_cot).astype(jnp.bfloat16)
    back_flat = back_rows.reshape(assigned, model_width)[rank]
    tokens_grad = jnp.sum(
        back_flat.reshape(token_count, top_count, model_width).astype(jnp.float32), axis=1
    )
    gates_grad = back_gate.reshape(-1)[rank].reshape(token_count, top_count)
    return (
        tokens_grad.astype(jnp.bfloat16),
        gates_grad,
        grad_w_gate[None],
        grad_w_up[None],
        grad_w_down[None],
    )

CORES = 2
ROW_TILE = 1024
FACTOR_ROWS = 128
PRODUCT_TILE = 1024
LANES = 128
HBM = pl.BlockSpec(memory_space=pltpu.HBM)
VMEM = pl.BlockSpec(memory_space=pltpu.VMEM)


def wait_for(copies):
    for copy in copies:
        copy.wait()


def tiles(count, size, body):
    @pl.loop(0, count // size)
    def _(i):
        body(pl.ds(pl.multiple_of(i * size, size), size))


def work_cost(rows, depth, width):
    return pl.CostEstimate(flops=60 * rows * depth * width, bytes_accessed=2 * rows * depth, transcendentals=0)


def step_kernel(lines, step, steps, passed, waited, token_count, model_width, f, *refs):
    refs = list(refs)
    take = lambda n: [refs.pop(0) for _ in range(n)]
    blocks, (pick_ref,) = take(lines), take(1)
    gate_w, up_w, down_w = take(CORES), take(CORES), take(CORES)
    if step:
        take(8)
    take(passed + waited)
    row_own, row_far = take(2)
    tok_all, cot_all = take(2)
    factor_all = take(6)
    mate_factors = take(1)[0] if step == steps - 1 else None
    take(passed)
    tok, cot, wg, wu, wd, pre_gate, pre_up, back, gg, gu = take(10)
    factors = take(6)
    in_sem, out_sem = take(2)
    rows = lines * token_count
    room = row_own.shape[1] - model_width

    slot = iter(range(64))
    copy_in = lambda src, dst: pltpu.make_async_copy(src, dst, in_sem.at[next(slot)])
    line_rows = [pl.ds(i * token_count, token_count) for i in range(lines)]
    columns = [pl.ds(e * f, f) for e in range(CORES)]
    padded = blocks[0].shape[1] - model_width
    first = [copy_in(blocks[i].at[:, pl.ds(0, model_width)], tok.at[line_rows[i]]) for i in range(lines)]
    first += [copy_in(gate_w[e], wg.at[:, columns[e]]) for e in range(CORES)]
    second = [copy_in(up_w[e], wu.at[:, columns[e]]) for e in range(CORES)]
    third = [copy_in(blocks[i].at[:, pl.ds(model_width, padded)], cot.at[line_rows[i]]) for i in range(lines)]
    third += [copy_in(down_w[e], wd.at[columns[e]]) for e in range(CORES)]
    for copy in first + second + third:
        copy.start()

    def gate_tile(c):
        pre_gate[:, c] = jnp.dot(tok[...], wg[:, c], preferred_element_type=jnp.float32)

    def up_tile(c):
        pre_up[:, c] = jnp.dot(tok[...], wu[:, c], preferred_element_type=jnp.float32)

    def back_tile(c):
        back[:, c] = contract_cols(cot[:, :model_width], wd[c, :])

    def factor_tile(line, r):
        gate_cols = jnp.dot(cot[r, model_width:], pick_ref[...], preferred_element_type=jnp.float32)
        sums = []
        for e in range(CORES):
            c = columns[e]
            gate, up, bh = pre_gate[r, c], pre_up[r, c], back[r, c]
            sigma = jax.nn.sigmoid(gate)
            active = gate * sigma
            prod = active * up
            hidden = prod.astype(jnp.bfloat16)
            sums.append(jnp.sum(hidden.astype(jnp.float32) * bh, axis=1, keepdims=True))
            weight = gate_cols[:, e : e + 1]
            scaled_back = weight * bh
            grad_gate = (scaled_back * up * sigma * (1.0 + gate * (1.0 - sigma))).astype(jnp.bfloat16)
            grad_up = (scaled_back * active).astype(jnp.bfloat16)
            gg[r, c] = grad_gate
            gu[r, c] = grad_up
            factors[e][r, :] = grad_gate
            factors[CORES + e][r, :] = grad_up
            factors[2 * CORES + e][r, :] = (weight * prod).astype(jnp.bfloat16)
        lane = lax.broadcasted_iota(jnp.int32, (sums[0].shape[0], room), 1)
        place = CORES * (step * lines + line)
        found = jnp.where(lane == place, sums[0], jnp.where(lane == place + 1, sums[1], 0.0))
        return found

    def own_terms(r):
        row_own[r, model_width:] = factor_tile(0, r)

    wait_for(first)
    tiles(CORES * f, CORES * f, gate_tile)
    wait_for(second)
    tiles(CORES * f, CORES * f, up_tile)
    wait_for(third)
    tiles(CORES * f, CORES * f, back_tile)
    tiles(token_count, FACTOR_ROWS, own_terms)
    for i in range(1, lines):

        @pl.loop(0, token_count // FACTOR_ROWS)
        def _(j):
            near = pl.ds(pl.multiple_of((i - 1) * token_count + j * FACTOR_ROWS, FACTOR_ROWS), FACTOR_ROWS)
            r = pl.ds(pl.multiple_of(i * token_count + j * FACTOR_ROWS, FACTOR_ROWS), FACTOR_ROWS)
            row_far[near, model_width:] = factor_tile(i, r).astype(jnp.bfloat16)

    at = pl.ds(step * rows, rows)
    outs = [(tok, tok_all), (cot.at[:, pl.ds(0, model_width)], cot_all)] + list(zip(factors, factor_all))
    pairs = [(a, b.at[at]) for a, b in outs]
    if mate_factors is not None:
        pairs += [(factors[CORES * i + 1], mate_factors.at[:, pl.ds(i * f, f)]) for i in range(3)]
    out_copies = [pltpu.make_async_copy(a, b, out_sem.at[i]) for i, (a, b) in enumerate(pairs)]
    for copy in out_copies:
        copy.start()

    def row_tile(c):
        grad = contract_cols(gg[...], wg[c, :]) + contract_cols(gu[...], wu[c, :])
        row_own[:, c] = grad[:token_count]
        row_far[:, c] = grad[token_count:].astype(jnp.bfloat16)

    tiles(model_width, ROW_TILE, row_tile)
    wait_for(out_copies)


def one_step(step, steps, blocks, pick, weights, held, passed=(), waited=()):
    lines = len(blocks)
    token_count = blocks[0].shape[0]
    model_width, f = weights[0].shape
    padded = blocks[0].shape[1] - model_width
    rows, wide = lines * token_count, CORES * f
    bf = jnp.bfloat16
    ins = [*blocks, pick, *weights, *held, *passed, *waited]
    whole = [jax.ShapeDtypeStruct((steps * rows, model_width), bf)] * 2
    whole += [jax.ShapeDtypeStruct((steps * rows, f), bf)] * 6
    out_shape = [
        jax.ShapeDtypeStruct((token_count, padded), jnp.float32),
        jax.ShapeDtypeStruct(((lines - 1) * token_count, padded), bf),
        *whole,
    ]
    if step == steps - 1:
        out_shape.append(jax.ShapeDtypeStruct((rows, 3 * f), bf))
    base = lines + 1 + len(weights)
    aliases = {base + i: 2 + i for i in range(len(held))}
    base += len(held)
    aliases |= {base + i: len(out_shape) + i for i in range(len(passed))}
    out_shape += [jax.ShapeDtypeStruct(value.shape, value.dtype) for value in passed]
    scratch = [pltpu.VMEM((rows, model_width), bf), pltpu.VMEM((rows, padded), bf)]
    scratch += [pltpu.VMEM((model_width, wide), bf)] * 2 + [pltpu.VMEM((wide, model_width), bf)]
    scratch += [pltpu.VMEM((rows, wide), jnp.float32)] * 3 + [pltpu.VMEM((rows, wide), bf)] * 2
    scratch += [pltpu.VMEM((rows, f), bf)] * 6
    scratch += [pltpu.SemaphoreType.DMA((2 * lines + 3 * CORES,)), pltpu.SemaphoreType.DMA((11,))]
    outs = pl.pallas_call(
        lambda *refs: step_kernel(lines, step, steps, len(passed), len(waited), token_count, model_width, f, *refs),
        out_shape=out_shape,
        in_specs=[HBM] * lines + [VMEM] + [HBM] * (len(ins) - lines - 1),
        out_specs=[VMEM] * 2 + [HBM] * (len(out_shape) - 2),
        scratch_shapes=scratch,
        input_output_aliases=aliases,
        compiler_params=pltpu.CompilerParams(vmem_limit_bytes=60 * 1024 * 1024),
        cost_estimate=work_cost(rows, model_width, 5 * wide),
    )(*ins)
    return outs[0], outs[1], list(outs[2:10]), outs[10:]


def mate_kernel(count, tok_ref, cot_ref, gate_ref, up_ref, hid_ref, out, tok, cot, pair, hid, sem):
    f = hid.shape[1]
    top = pl.ds(0, count)
    first = [(gate_ref, pair.at[:, pl.ds(0, f)]), (up_ref, pair.at[:, pl.ds(f, f)]), (tok_ref, tok)]
    moves = first + [(hid_ref, hid), (cot_ref, cot)]
    copies = [pltpu.make_async_copy(src.at[top], dst, sem.at[i]) for i, (src, dst) in enumerate(moves)]
    for copy in copies:
        copy.start()

    def pair_tile(c):
        out[: 2 * f, c] = contract_rows(pair[...], tok[:, c]).astype(jnp.bfloat16)

    def down_tile(c):
        out[2 * f :, c] = contract_rows(hid[...], cot[:, c]).astype(jnp.bfloat16)

    wait_for(copies[:3])
    tiles(tok.shape[1], PRODUCT_TILE, pair_tile)
    wait_for(copies[3:])
    tiles(tok.shape[1], PRODUCT_TILE, down_tile)


def mate_products(count, tok, cot, gate, up, hid):
    model_width, f = tok.shape[1], gate.shape[1]
    bf = jnp.bfloat16
    return pl.pallas_call(
        lambda *refs: mate_kernel(count, *refs),
        out_shape=jax.ShapeDtypeStruct((3 * f, model_width), bf),
        in_specs=[HBM] * 5,
        out_specs=VMEM,
        scratch_shapes=[
            pltpu.VMEM((count, model_width), bf),
            pltpu.VMEM((count, model_width), bf),
            pltpu.VMEM((count, 2 * f), bf),
            pltpu.VMEM((count, f), bf),
            pltpu.SemaphoreType.DMA((5,)),
        ],
        compiler_params=pltpu.CompilerParams(vmem_limit_bytes=60 * 1024 * 1024),
        cost_estimate=work_cost(count, model_width, 3 * f),
    )(tok, cot, gate, up, hid)


def finish_kernel(lines, tok_ref, cot_ref, gate_ref, up_ref, hid_ref, got_ref, factor_ref, *refs):
    far_blocks = refs[:lines]
    gate_out, up_out, down_out, tok, cot, pair, hid, got, sem = refs[lines + 1 :]
    rows, model_width = tok_ref.shape
    f = gate_ref.shape[1]
    token_count = far_blocks[0].shape[0]
    near, far = pl.ds(0, rows), pl.ds(rows, lines * token_count)
    line = [pl.ds(rows + i * token_count, token_count) for i in range(lines)]
    first = [(gate_ref, pair.at[near, pl.ds(0, f)]), (up_ref, pair.at[near, pl.ds(f, f)]), (tok_ref, tok.at[near])]
    first += [(factor_ref.at[:, pl.ds(0, 2 * f)], pair.at[far]), (got_ref, got)]
    first += [(far_blocks[i].at[:, pl.ds(0, model_width)], tok.at[line[i]]) for i in range(lines)]
    second = [(hid_ref, hid.at[near]), (factor_ref.at[:, pl.ds(2 * f, f)], hid.at[far]), (cot_ref, cot.at[near])]
    second += [(far_blocks[i].at[:, pl.ds(model_width, model_width)], cot.at[line[i]]) for i in range(lines)]
    copies = [pltpu.make_async_copy(src, dst, sem.at[i]) for i, (src, dst) in enumerate(first + second)]
    for copy in copies:
        copy.start()

    def pair_tile(c):
        both = contract_rows(pair[...], tok[:, c])
        both = (both + got[: 2 * f, c].astype(jnp.float32)).astype(jnp.bfloat16).T
        gate_out[c, :] = both[:, :f]
        up_out[c, :] = both[:, f:]

    def down_tile(c):
        down = contract_rows(hid[...], cot[:, c])
        down_out[:, c] = (down + got[2 * f :, c].astype(jnp.float32)).astype(jnp.bfloat16)

    wait_for(copies[: len(first)])
    tiles(model_width, PRODUCT_TILE, pair_tile)
    wait_for(copies[len(first) :])
    tiles(model_width, PRODUCT_TILE, down_tile)


def finish(tok, cot, gate, up, hid, got, far_factors, far_blocks, waited):
    rows, model_width = tok.shape
    f = gate.shape[1]
    lines = len(far_blocks)
    more = rows + lines * far_blocks[0].shape[0]
    bf = jnp.bfloat16
    ins = [tok, cot, gate, up, hid, got, far_factors, *far_blocks, waited]
    return pl.pallas_call(
        lambda *refs: finish_kernel(lines, *refs),
        out_shape=[jax.ShapeDtypeStruct((model_width, f), bf)] * 2 + [jax.ShapeDtypeStruct((f, model_width), bf)],
        in_specs=[HBM] * len(ins),
        out_specs=[VMEM] * 3,
        scratch_shapes=[
            pltpu.VMEM((more, model_width), bf),
            pltpu.VMEM((more, model_width), bf),
            pltpu.VMEM((more, 2 * f), bf),
            pltpu.VMEM((more, f), bf),
            pltpu.VMEM((3 * f, model_width), bf),
            pltpu.SemaphoreType.DMA((8 + 2 * lines,)),
        ],
        compiler_params=pltpu.CompilerParams(vmem_limit_bytes=60 * 1024 * 1024),
        cost_estimate=work_cost(more, model_width, 3 * f),
    )(*ins)


def gathered(tokens, cotangent, expert_ids, gates, w_gate, w_up, w_down):
    z_count = lax.axis_size("expert")
    dp_count = lax.axis_size("dp")
    x_count = dp_count // CORES
    expert_count = z_count * dp_count
    token_count, model_width = tokens.shape
    z_here = lax.axis_index("expert")
    dp_here = lax.axis_index("dp")

    def z_shift(value, step):
        return lax.ppermute(value, "expert", [(i, (i + step) % z_count) for i in range(z_count)])

    def x_shift(value, step):
        return lax.ppermute(value, "dp", [(i, (i + CORES * step) % dp_count) for i in range(dp_count)])

    def core_swap(value):
        return lax.ppermute(value, "dp", [(i, i ^ 1) for i in range(dp_count)])

    def after(value, *earlier):
        return lax.optimization_barrier((value, *earlier))[0]

    def across(block):
        return [block] + [x_shift(block, s) for s in range(1, x_count)]

    def home(d, carried=None):
        line = row_own[d]
        for s in range(1, x_count):
            line = line + x_shift(row_far[d][s - 1], x_count - s).astype(jnp.float32)
        if carried is not None:
            line = line + carried.astype(jnp.float32)
        return line.astype(jnp.bfloat16) if d else line

    expert_range = jnp.arange(expert_count, dtype=jnp.int32)
    chosen = expert_ids[:, :, None] == expert_range
    gate_table = jnp.sum(jnp.where(chosen, gates[:, :, None].astype(jnp.float32), 0.0), axis=1).astype(jnp.bfloat16)
    table_width = -(-expert_count // LANES) * LANES
    gate_table = jnp.pad(gate_table, ((0, 0), (0, table_width - expert_count)))
    block = jnp.concatenate([tokens, cotangent, gate_table], axis=1)
    own_expert = z_here * dp_count + dp_here
    mate_expert = z_here * dp_count + (dp_here ^ 1)
    pick_row = jnp.arange(table_width, dtype=jnp.int32)[:, None]
    pick_column = jnp.arange(LANES, dtype=jnp.int32)[None, :]
    wanted = jnp.where(pick_column == 0, own_expert, mate_expert)
    pick = ((pick_row == wanted) & (pick_column < CORES)).astype(jnp.bfloat16)

    weights = []
    for own in (w_gate[0], w_up[0], w_down[0]):
        weights += [own, core_swap(own)]
    ring = z_shift(block, 1)
    pairs = [across(block)]
    ring = after(ring, *weights[1::2])

    row_own, row_far, held, line = [], [], [], tokens
    mate = jnp.zeros((3 * w_gate.shape[2], model_width), jnp.bfloat16)
    for d in range(z_count):
        ready = []
        if d + 1 < z_count:
            pairs.append(across(ring))
            following = z_shift(ring, 1) if d + 2 < z_count else None
            ready = [ring]
        passed, waited = [], []
        if d and d + 1 == z_count:
            count = d * x_count * token_count
            mate = mate_products(count, held[0], held[1], held[3], held[5], held[7])
            passed, waited = ([row_far[0][0], row_own[1]] if d > 1 else [row_far[0][0]]), [mate]
        outs = one_step(d, z_count, pairs[d], after(pick, *ready), weights, held, passed, waited)
        own, far, held, mate_factors = outs
        if len(mate_factors) > 1:
            row_far[0] = mate_factors[1][None]
        if len(mate_factors) > 2:
            row_own[1] = mate_factors[2]
        if d + 1 < z_count:
            far = after(far, pairs[d + 1][-1])
        if d + 2 < z_count:
            ring = after(following, far)
        row_own.append(own)
        row_far.append(far.reshape(x_count - 1, token_count, -1))

    carried = None
    for d in range(1, z_count):
        line = home(d, carried)
        carried = z_shift(line, 1)
    got = core_swap(mate)
    far_blocks = [core_swap(block) for block in pairs[-1]]
    far_factors = core_swap(mate_factors[0])
    grads = finish(held[0], held[1], held[2], held[4], held[6], got, far_factors, far_blocks, line)

    row_own[0] = after(row_own[0], grads[0])
    total = home(0, carried)
    tokens_grad = total[:, :model_width].astype(jnp.bfloat16)
    back = total[:, model_width : model_width + expert_count]
    column_ids = []
    for d in range(z_count):
        for s in range(x_count):
            dp_from = (dp_here + CORES * s) % dp_count
            first = ((z_here + d) % z_count) * dp_count
            column_ids += [first + dp_from, first + (dp_from ^ 1)]
    same = expert_ids[:, :, None] == jnp.stack(column_ids)
    gates_grad = jnp.sum(jnp.where(same, back[:, None, :], 0.0), axis=2).astype(jnp.bfloat16)
    return (tokens_grad, gates_grad, *[g[None] for g in grads])


def per_device(tokens, cotangent, expert_ids, gates, w_gate, w_up, w_down):
    expert_count = lax.axis_size("expert") * lax.axis_size("dp")
    plan = gathered if expert_count <= 4 * expert_ids.shape[1] and lax.axis_size("dp") % CORES == 0 else dispatched
    return plan(tokens, cotangent, expert_ids, gates, w_gate, w_up, w_down)


def solution(mesh):
    placed = (
        P(("group", "expert", "dp"), None),
        P(("group", "expert", "dp"), None),
        P(("group", "expert", "dp"), None),
        P(("group", "expert", "dp"), None),
        P(("expert", "dp"), None, None),
        P(("expert", "dp"), None, None),
        P(("expert", "dp"), None, None),
    )
    return jax.shard_map(
        per_device,
        mesh=mesh,
        in_specs=placed,
        out_specs=(
            P(("group", "expert", "dp"), None),
            P(("group", "expert", "dp"), None),
            P(("group", "expert", "dp"), None, None),
            P(("group", "expert", "dp"), None, None),
            P(("group", "expert", "dp"), None, None),
        ),
        check_vma=False,
    )
```

```python
import jax
import jax.numpy as jnp
from jax import lax
from jax.experimental import pallas as pl
from jax.experimental.pallas import tpu as pltpu
from jax.sharding import PartitionSpec as P


def contract_rows(left, right):
    return lax.dot_general(
        left, right, (((0,), (0,)), ((), ())), preferred_element_type=jnp.float32
    )


def contract_cols(left, right):
    return lax.dot_general(
        left, right, (((1,), (1,)), ((), ())), preferred_element_type=jnp.float32
    )


def expert_math(rows_in, rows_cot, row_gate, w_one, u_one, d_one):
    pre_gate = jnp.dot(rows_in, w_one, preferred_element_type=jnp.float32)
    pre_up = jnp.dot(rows_in, u_one, preferred_element_type=jnp.float32)
    sigma = jax.nn.sigmoid(pre_gate)
    active = pre_gate * sigma
    hidden = (active * pre_up).astype(jnp.bfloat16)
    back_hidden = contract_cols(rows_cot, d_one)
    expert_out = jnp.dot(hidden, d_one, preferred_element_type=jnp.float32)
    gate_term = jnp.sum(rows_cot.astype(jnp.float32) * expert_out, axis=1)
    weight_col = row_gate.astype(jnp.float32)[:, None]
    scaled_back = weight_col * back_hidden
    grad_pre_gate = (scaled_back * pre_up * sigma * (1.0 + pre_gate * (1.0 - sigma))).astype(
        jnp.bfloat16
    )
    grad_pre_up = (scaled_back * active).astype(jnp.bfloat16)
    scaled_hidden = (weight_col * active * pre_up).astype(jnp.bfloat16)
    row_grad = (contract_cols(grad_pre_gate, w_one) + contract_cols(grad_pre_up, u_one)).astype(
        jnp.bfloat16
    )
    return (row_grad, gate_term.astype(jnp.bfloat16), grad_pre_gate, grad_pre_up, scaled_hidden)


def dispatched(tokens, cotangent, expert_ids, gates, w_gate, w_up, w_down):
    token_count = tokens.shape[0]
    model_width = tokens.shape[1]
    top_count = expert_ids.shape[1]
    expert_count = lax.axis_size("expert") * lax.axis_size("dp")
    assigned = token_count * top_count
    slot_count = assigned // expert_count
    position = jnp.arange(assigned, dtype=jnp.int32)
    order = jnp.argsort(expert_ids.reshape(-1) * assigned + position)
    rank = jnp.zeros((assigned,), jnp.int32).at[order].set(position)
    source = order // top_count
    send_in = tokens[source].reshape(expert_count, slot_count, model_width)
    send_cot = cotangent[source].reshape(expert_count, slot_count, model_width)
    send_gate = gates.reshape(-1)[order].reshape(expert_count, slot_count)
    w_one = w_gate[0]
    u_one = w_up[0]
    d_one = w_down[0]
    rows_in = lax.all_to_all(send_in, ("expert", "dp"), split_axis=0, concat_axis=0, tiled=True)
    rows_cot = lax.all_to_all(send_cot, ("expert", "dp"), split_axis=0, concat_axis=0, tiled=True)
    row_gate = lax.all_to_all(send_gate, ("expert", "dp"), split_axis=0, concat_axis=0, tiled=True)
    senders = rows_in.shape[0]
    width_slots = rows_in.shape[1]
    outputs = expert_math(
        rows_in.reshape(-1, model_width),
        rows_cot.reshape(-1, model_width),
        row_gate.reshape(-1),
        w_one,
        u_one,
        d_one,
    )
    back_rows = lax.all_to_all(
        outputs[0].reshape(senders, width_slots, model_width),
        ("expert", "dp"),
        split_axis=0,
        concat_axis=0,
        tiled=True,
    )
    back_gate = lax.all_to_all(
        outputs[1].reshape(senders, width_slots),
        ("expert", "dp"),
        split_axis=0,
        concat_axis=0,
        tiled=True,
    )
    results = (
        back_rows,
        back_gate,
        rows_in,
        rows_cot,
        outputs[2].reshape(senders, width_slots, -1),
        outputs[3].reshape(senders, width_slots, -1),
        outputs[4].reshape(senders, width_slots, -1),
    )
    back_rows, back_gate, recv_in, recv_cot, grad_pre_gate, grad_pre_up, scaled_hidden = results
    recv_in = recv_in.reshape(-1, model_width)
    recv_cot = recv_cot.reshape(-1, model_width)
    grad_pre_gate = grad_pre_gate.reshape(assigned, -1)
    grad_pre_up = grad_pre_up.reshape(assigned, -1)
    scaled_hidden = scaled_hidden.reshape(assigned, -1)
    grad_w_gate = contract_rows(recv_in, grad_pre_gate).astype(jnp.bfloat16)
    grad_w_up = contract_rows(recv_in, grad_pre_up).astype(jnp.bfloat16)
    grad_w_down = contract_rows(scaled_hidden, recv_cot).astype(jnp.bfloat16)
    back_flat = back_rows.reshape(assigned, model_width)[rank]
    tokens_grad = jnp.sum(
        back_flat.reshape(token_count, top_count, model_width).astype(jnp.float32), axis=1
    )
    gates_grad = back_gate.reshape(-1)[rank].reshape(token_count, top_count)
    return (
        tokens_grad.astype(jnp.bfloat16),
        gates_grad,
        grad_w_gate[None],
        grad_w_up[None],
        grad_w_down[None],
    )

CORES = 2
ROW_TILE = 1024
FACTOR_ROWS = 128
PRODUCT_TILE = 1024
LANES = 128
HBM = pl.BlockSpec(memory_space=pltpu.HBM)
VMEM = pl.BlockSpec(memory_space=pltpu.VMEM)


def wait_for(copies):
    for copy in copies:
        copy.wait()


def tiles(count, size, body):
    @pl.loop(0, count // size)
    def _(i):
        body(pl.ds(pl.multiple_of(i * size, size), size))


def work_cost(rows, depth, width):
    return pl.CostEstimate(flops=60 * rows * depth * width, bytes_accessed=2 * rows * depth, transcendentals=0)


def step_kernel(lines, step, steps, passed, waited, token_count, model_width, f, *refs):
    refs = list(refs)
    take = lambda n: [refs.pop(0) for _ in range(n)]
    blocks, (pick_ref,) = take(lines), take(1)
    gate_w, up_w, down_w = take(CORES), take(CORES), take(CORES)
    if step:
        take(8)
    take(passed + waited)
    row_own, row_far = take(2)
    tok_all, cot_all = take(2)
    factor_all = take(6)
    mate_factors = take(1)[0] if step == steps - 1 else None
    take(passed)
    tok, cot, wg, wu, wd, pre_gate, pre_up, back, gg, gu = take(10)
    factors = take(6)
    in_sem, out_sem = take(2)
    rows = lines * token_count
    room = row_own.shape[1] - model_width

    slot = iter(range(64))
    copy_in = lambda src, dst: pltpu.make_async_copy(src, dst, in_sem.at[next(slot)])
    line_rows = [pl.ds(i * token_count, token_count) for i in range(lines)]
    columns = [pl.ds(e * f, f) for e in range(CORES)]
    padded = blocks[0].shape[1] - model_width
    first = [copy_in(blocks[i].at[:, pl.ds(0, model_width)], tok.at[line_rows[i]]) for i in range(lines)]
    first += [copy_in(gate_w[e], wg.at[:, columns[e]]) for e in range(CORES)]
    second = [copy_in(up_w[e], wu.at[:, columns[e]]) for e in range(CORES)]
    third = [copy_in(blocks[i].at[:, pl.ds(model_width, padded)], cot.at[line_rows[i]]) for i in range(lines)]
    third += [copy_in(down_w[e], wd.at[columns[e]]) for e in range(CORES)]
    for copy in first + second + third:
        copy.start()

    def gate_tile(c):
        pre_gate[:, c] = jnp.dot(tok[...], wg[:, c], preferred_element_type=jnp.float32)

    def up_tile(c):
        pre_up[:, c] = jnp.dot(tok[...], wu[:, c], preferred_element_type=jnp.float32)

    def back_tile(c):
        back[:, c] = contract_cols(cot[:, :model_width], wd[c, :])

    def factor_tile(line, r):
        gate_cols = jnp.dot(cot[r, model_width:], pick_ref[...], preferred_element_type=jnp.float32)
        sums = []
        for e in range(CORES):
            c = columns[e]
            gate, up, bh = pre_gate[r, c], pre_up[r, c], back[r, c]
            sigma = jax.nn.sigmoid(gate)
            active = gate * sigma
            prod = active * up
            hidden = prod.astype(jnp.bfloat16)
            sums.append(jnp.sum(hidden.astype(jnp.float32) * bh, axis=1, keepdims=True))
            weight = gate_cols[:, e : e + 1]
            scaled_back = weight * bh
            grad_gate = (scaled_back * up * sigma * (1.0 + gate * (1.0 - sigma))).astype(jnp.bfloat16)
            grad_up = (scaled_back * active).astype(jnp.bfloat16)
            gg[r, c] = grad_gate
            gu[r, c] = grad_up
            factors[e][r, :] = grad_gate
            factors[CORES + e][r, :] = grad_up
            factors[2 * CORES + e][r, :] = (weight * prod).astype(jnp.bfloat16)
        lane = lax.broadcasted_iota(jnp.int32, (sums[0].shape[0], room), 1)
        place = CORES * (step * lines + line)
        found = jnp.where(lane == place, sums[0], jnp.where(lane == place + 1, sums[1], 0.0))
        return found

    def own_terms(r):
        row_own[r, model_width:] = factor_tile(0, r)

    wait_for(first)
    tiles(CORES * f, CORES * f, gate_tile)
    wait_for(second)
    tiles(CORES * f, CORES * f, up_tile)
    wait_for(third)
    tiles(CORES * f, CORES * f, back_tile)
    tiles(token_count, FACTOR_ROWS, own_terms)
    for i in range(1, lines):

        @pl.loop(0, token_count // FACTOR_ROWS)
        def _(j):
            near = pl.ds(pl.multiple_of((i - 1) * token_count + j * FACTOR_ROWS, FACTOR_ROWS), FACTOR_ROWS)
            r = pl.ds(pl.multiple_of(i * token_count + j * FACTOR_ROWS, FACTOR_ROWS), FACTOR_ROWS)
            row_far[near, model_width:] = factor_tile(i, r).astype(jnp.bfloat16)

    at = pl.ds(step * rows, rows)
    outs = [(tok, tok_all), (cot.at[:, pl.ds(0, model_width)], cot_all)] + list(zip(factors, factor_all))
    pairs = [(a, b.at[at]) for a, b in outs]
    if mate_factors is not None:
        pairs += [(factors[CORES * i + 1], mate_factors.at[:, pl.ds(i * f, f)]) for i in range(3)]
    out_copies = [pltpu.make_async_copy(a, b, out_sem.at[i]) for i, (a, b) in enumerate(pairs)]
    for copy in out_copies:
        copy.start()

    def row_tile(c):
        grad = contract_cols(gg[...], wg[c, :]) + contract_cols(gu[...], wu[c, :])
        row_own[:, c] = grad[:token_count]
        row_far[:, c] = grad[token_count:].astype(jnp.bfloat16)

    tiles(model_width, ROW_TILE, row_tile)
    wait_for(out_copies)


def one_step(step, steps, blocks, pick, weights, held, passed=(), waited=()):
    lines = len(blocks)
    token_count = blocks[0].shape[0]
    model_width, f = weights[0].shape
    padded = blocks[0].shape[1] - model_width
    rows, wide = lines * token_count, CORES * f
    bf = jnp.bfloat16
    ins = [*blocks, pick, *weights, *held, *passed, *waited]
    whole = [jax.ShapeDtypeStruct((steps * rows, model_width), bf)] * 2
    whole += [jax.ShapeDtypeStruct((steps * rows, f), bf)] * 6
    out_shape = [
        jax.ShapeDtypeStruct((token_count, padded), jnp.float32),
        jax.ShapeDtypeStruct(((lines - 1) * token_count, padded), bf),
        *whole,
    ]
    if step == steps - 1:
        out_shape.append(jax.ShapeDtypeStruct((rows, 3 * f), bf))
    base = lines + 1 + len(weights)
    aliases = {base + i: 2 + i for i in range(len(held))}
    base += len(held)
    aliases |= {base + i: len(out_shape) + i for i in range(len(passed))}
    out_shape += [jax.ShapeDtypeStruct(value.shape, value.dtype) for value in passed]
    scratch = [pltpu.VMEM((rows, model_width), bf), pltpu.VMEM((rows, padded), bf)]
    scratch += [pltpu.VMEM((model_width, wide), bf)] * 2 + [pltpu.VMEM((wide, model_width), bf)]
    scratch += [pltpu.VMEM((rows, wide), jnp.float32)] * 3 + [pltpu.VMEM((rows, wide), bf)] * 2
    scratch += [pltpu.VMEM((rows, f), bf)] * 6
    scratch += [pltpu.SemaphoreType.DMA((2 * lines + 3 * CORES,)), pltpu.SemaphoreType.DMA((11,))]
    outs = pl.pallas_call(
        lambda *refs: step_kernel(lines, step, steps, len(passed), len(waited), token_count, model_width, f, *refs),
        out_shape=out_shape,
        in_specs=[HBM] * lines + [VMEM] + [HBM] * (len(ins) - lines - 1),
        out_specs=[VMEM] * 2 + [HBM] * (len(out_shape) - 2),
        scratch_shapes=scratch,
        input_output_aliases=aliases,
        compiler_params=pltpu.CompilerParams(vmem_limit_bytes=60 * 1024 * 1024),
        cost_estimate=work_cost(rows, model_width, 5 * wide),
    )(*ins)
    return outs[0], outs[1], list(outs[2:10]), outs[10:]


def mate_kernel(count, tok_ref, cot_ref, gate_ref, up_ref, hid_ref, out, tok, cot, pair, hid, sem):
    f = hid.shape[1]
    top = pl.ds(0, count)
    first = [(gate_ref, pair.at[:, pl.ds(0, f)]), (up_ref, pair.at[:, pl.ds(f, f)]), (tok_ref, tok)]
    moves = first + [(hid_ref, hid), (cot_ref, cot)]
    copies = [pltpu.make_async_copy(src.at[top], dst, sem.at[i]) for i, (src, dst) in enumerate(moves)]
    for copy in copies:
        copy.start()

    def pair_tile(c):
        out[: 2 * f, c] = contract_rows(pair[...], tok[:, c]).astype(jnp.bfloat16)

    def down_tile(c):
        out[2 * f :, c] = contract_rows(hid[...], cot[:, c]).astype(jnp.bfloat16)

    wait_for(copies[:3])
    tiles(tok.shape[1], PRODUCT_TILE, pair_tile)
    wait_for(copies[3:])
    tiles(tok.shape[1], PRODUCT_TILE, down_tile)


def mate_products(count, tok, cot, gate, up, hid):
    model_width, f = tok.shape[1], gate.shape[1]
    bf = jnp.bfloat16
    return pl.pallas_call(
        lambda *refs: mate_kernel(count, *refs),
        out_shape=jax.ShapeDtypeStruct((3 * f, model_width), bf),
        in_specs=[HBM] * 5,
        out_specs=VMEM,
        scratch_shapes=[
            pltpu.VMEM((count, model_width), bf),
            pltpu.VMEM((count, model_width), bf),
            pltpu.VMEM((count, 2 * f), bf),
            pltpu.VMEM((count, f), bf),
            pltpu.SemaphoreType.DMA((5,)),
        ],
        compiler_params=pltpu.CompilerParams(vmem_limit_bytes=60 * 1024 * 1024),
        cost_estimate=work_cost(count, model_width, 3 * f),
    )(tok, cot, gate, up, hid)


def finish_kernel(lines, tok_ref, cot_ref, gate_ref, up_ref, hid_ref, got_ref, factor_ref, *refs):
    far_blocks = refs[:lines]
    gate_out, up_out, down_out, tok, cot, pair, hid, got, sem = refs[lines + 1 :]
    rows, model_width = tok_ref.shape
    f = gate_ref.shape[1]
    token_count = far_blocks[0].shape[0]
    near, far = pl.ds(0, rows), pl.ds(rows, lines * token_count)
    line = [pl.ds(rows + i * token_count, token_count) for i in range(lines)]
    first = [(gate_ref, pair.at[near, pl.ds(0, f)]), (up_ref, pair.at[near, pl.ds(f, f)]), (tok_ref, tok.at[near])]
    first += [(factor_ref.at[:, pl.ds(0, 2 * f)], pair.at[far]), (got_ref, got)]
    first += [(far_blocks[i].at[:, pl.ds(0, model_width)], tok.at[line[i]]) for i in range(lines)]
    second = [(hid_ref, hid.at[near]), (factor_ref.at[:, pl.ds(2 * f, f)], hid.at[far]), (cot_ref, cot.at[near])]
    second += [(far_blocks[i].at[:, pl.ds(model_width, model_width)], cot.at[line[i]]) for i in range(lines)]
    copies = [pltpu.make_async_copy(src, dst, sem.at[i]) for i, (src, dst) in enumerate(first + second)]
    for copy in copies:
        copy.start()

    def pair_tile(c):
        both = contract_rows(pair[...], tok[:, c])
        both = (both + got[: 2 * f, c].astype(jnp.float32)).astype(jnp.bfloat16).T
        gate_out[c, :] = both[:, :f]
        up_out[c, :] = both[:, f:]

    def down_tile(c):
        down = contract_rows(hid[...], cot[:, c])
        down_out[:, c] = (down + got[2 * f :, c].astype(jnp.float32)).astype(jnp.bfloat16)

    wait_for(copies[: len(first)])
    tiles(model_width, PRODUCT_TILE, pair_tile)
    wait_for(copies[len(first) :])
    tiles(model_width, PRODUCT_TILE, down_tile)


def finish(tok, cot, gate, up, hid, got, far_factors, far_blocks, waited):
    rows, model_width = tok.shape
    f = gate.shape[1]
    lines = len(far_blocks)
    more = rows + lines * far_blocks[0].shape[0]
    bf = jnp.bfloat16
    ins = [tok, cot, gate, up, hid, got, far_factors, *far_blocks, waited]
    return pl.pallas_call(
        lambda *refs: finish_kernel(lines, *refs),
        out_shape=[jax.ShapeDtypeStruct((model_width, f), bf)] * 2 + [jax.ShapeDtypeStruct((f, model_width), bf)],
        in_specs=[HBM] * len(ins),
        out_specs=[VMEM] * 3,
        scratch_shapes=[
            pltpu.VMEM((more, model_width), bf),
            pltpu.VMEM((more, model_width), bf),
            pltpu.VMEM((more, 2 * f), bf),
            pltpu.VMEM((more, f), bf),
            pltpu.VMEM((3 * f, model_width), bf),
            pltpu.SemaphoreType.DMA((8 + 2 * lines,)),
        ],
        compiler_params=pltpu.CompilerParams(vmem_limit_bytes=60 * 1024 * 1024),
        cost_estimate=work_cost(more, model_width, 3 * f),
    )(*ins)


def pack_kernel(tok_ref, cot_ref, ids_ref, gates_ref, out, table, sem):
    model_width = tok_ref.shape[1]
    token_count, room = table.shape
    moves = [(tok_ref, 0, model_width), (cot_ref, model_width, model_width), (table, 2 * model_width, room)]
    copies = [
        pltpu.make_async_copy(src, out.at[:, pl.ds(start, width)], sem.at[i])
        for i, (src, start, width) in enumerate(moves)
    ]
    copies[0].start()
    copies[1].start()
    expert = lax.broadcasted_iota(jnp.int32, (room, token_count), 0)
    found = jnp.zeros((room, token_count), jnp.float32)
    for k in range(ids_ref.shape[0]):
        found = found + jnp.where(expert == ids_ref[k : k + 1, :], gates_ref[k : k + 1, :].astype(jnp.float32), 0.0)
    table[...] = found.T.astype(jnp.bfloat16)
    copies[2].start()
    wait_for(copies)


def pack(tokens, cotangent, expert_ids, gates, room):
    token_count, model_width = tokens.shape
    return pl.pallas_call(
        pack_kernel,
        out_shape=jax.ShapeDtypeStruct((token_count, 2 * model_width + room), jnp.bfloat16),
        in_specs=[VMEM, VMEM, VMEM, VMEM],
        out_specs=HBM,
        scratch_shapes=[pltpu.VMEM((token_count, room), jnp.bfloat16), pltpu.SemaphoreType.DMA((3,))],
        compiler_params=pltpu.CompilerParams(vmem_limit_bytes=60 * 1024 * 1024),
    )(tokens, cotangent, expert_ids.T, gates.T)


def gathered(tokens, cotangent, expert_ids, gates, w_gate, w_up, w_down):
    z_count = lax.axis_size("expert")
    dp_count = lax.axis_size("dp")
    x_count = dp_count // CORES
    expert_count = z_count * dp_count
    token_count, model_width = tokens.shape
    z_here = lax.axis_index("expert")
    dp_here = lax.axis_index("dp")

    def z_shift(value, step):
        return lax.ppermute(value, "expert", [(i, (i + step) % z_count) for i in range(z_count)])

    def x_shift(value, step):
        return lax.ppermute(value, "dp", [(i, (i + CORES * step) % dp_count) for i in range(dp_count)])

    def core_swap(value):
        return lax.ppermute(value, "dp", [(i, i ^ 1) for i in range(dp_count)])

    def after(value, *earlier):
        return lax.optimization_barrier((value, *earlier))[0]

    def across(block):
        return [block] + [x_shift(block, s) for s in range(1, x_count)]

    def home(d, carried=None):
        line = row_own[d]
        for s in range(1, x_count):
            line = line + x_shift(row_far[d][s - 1], x_count - s).astype(jnp.float32)
        if carried is not None:
            line = line + carried.astype(jnp.float32)
        return line.astype(jnp.bfloat16) if d else line

    table_width = -(-expert_count // LANES) * LANES
    block = pack(tokens, cotangent, expert_ids, gates, table_width)
    own_expert = z_here * dp_count + dp_here
    mate_expert = z_here * dp_count + (dp_here ^ 1)
    pick_row = jnp.arange(table_width, dtype=jnp.int32)[:, None]
    pick_column = jnp.arange(LANES, dtype=jnp.int32)[None, :]
    wanted = jnp.where(pick_column == 0, own_expert, mate_expert)
    pick = ((pick_row == wanted) & (pick_column < CORES)).astype(jnp.bfloat16)

    weights = []
    for own in (w_gate[0], w_up[0], w_down[0]):
        weights += [own, core_swap(own)]
    ring = z_shift(block, 1)
    pairs = [across(block)]
    ring = after(ring, *weights[1::2])

    row_own, row_far, held, line, carried = [], [], [], tokens, None
    mate = jnp.zeros((3 * w_gate.shape[2], model_width), jnp.bfloat16)
    for d in range(z_count):
        ready = []
        if d + 1 < z_count:
            if d > 1 and d + 2 == z_count:
                pairs.append([ring] + [z_shift(block, 1) for block in pairs[d][1:]])
            else:
                pairs.append(across(ring))
            following = z_shift(ring, 1) if d + 2 < z_count else None
            ready = [ring]
        passed, waited = [], []
        if d and d + 1 == z_count:
            count = d * x_count * token_count
            mate = mate_products(count, held[0], held[1], held[3], held[5], held[7])
            passed, waited = [row_far[0][0]], [mate]
            if d > 1:
                carried = home(1)
                waited.append(carried)
                carried = z_shift(carried, 1)
        outs = one_step(d, z_count, pairs[d], after(pick, *ready), weights, held, passed, waited)
        own, far, held, mate_factors = outs
        if len(mate_factors) > 1:
            row_far[0] = mate_factors[1][None]
        if d + 1 < z_count:
            far = after(far, pairs[d + 1][-1])
        if d + 2 < z_count:
            ring = after(following, far)
        row_own.append(own)
        row_far.append(far.reshape(x_count - 1, token_count, -1))

    for d in range(1 if carried is None else 2, z_count):
        line = home(d, carried)
        carried = z_shift(line, 1)
    got = core_swap(mate)
    far_blocks = [core_swap(block) for block in pairs[-1]]
    far_factors = core_swap(mate_factors[0])
    grads = finish(held[0], held[1], held[2], held[4], held[6], got, far_factors, far_blocks, line)

    row_own[0] = after(row_own[0], grads[0])
    total = home(0, carried)
    tokens_grad = total[:, :model_width].astype(jnp.bfloat16)
    back = total[:, model_width : model_width + expert_count]
    column_ids = []
    for d in range(z_count):
        for s in range(x_count):
            dp_from = (dp_here + CORES * s) % dp_count
            first = ((z_here + d) % z_count) * dp_count
            column_ids += [first + dp_from, first + (dp_from ^ 1)]
    same = expert_ids[:, :, None] == jnp.stack(column_ids)
    gates_grad = jnp.sum(jnp.where(same, back[:, None, :], 0.0), axis=2).astype(jnp.bfloat16)
    return (tokens_grad, gates_grad, *[g[None] for g in grads])


def per_device(tokens, cotangent, expert_ids, gates, w_gate, w_up, w_down):
    expert_count = lax.axis_size("expert") * lax.axis_size("dp")
    plan = gathered if expert_count <= 4 * expert_ids.shape[1] and lax.axis_size("dp") % CORES == 0 else dispatched
    return plan(tokens, cotangent, expert_ids, gates, w_gate, w_up, w_down)


def solution(mesh):
    placed = (
        P(("group", "expert", "dp"), None),
        P(("group", "expert", "dp"), None),
        P(("group", "expert", "dp"), None),
        P(("group", "expert", "dp"), None),
        P(("expert", "dp"), None, None),
        P(("expert", "dp"), None, None),
        P(("expert", "dp"), None, None),
    )
    return jax.shard_map(
        per_device,
        mesh=mesh,
        in_specs=placed,
        out_specs=(
            P(("group", "expert", "dp"), None),
            P(("group", "expert", "dp"), None),
            P(("group", "expert", "dp"), None, None),
            P(("group", "expert", "dp"), None, None),
            P(("group", "expert", "dp"), None, None),
        ),
        check_vma=False,
    )
```

```python
import jax
import jax.numpy as jnp
from jax import lax
from jax.experimental import pallas as pl
from jax.experimental.pallas import tpu as pltpu
from jax.sharding import PartitionSpec as P


def contract_rows(left, right):
    return lax.dot_general(
        left, right, (((0,), (0,)), ((), ())), preferred_element_type=jnp.float32
    )


def contract_cols(left, right):
    return lax.dot_general(
        left, right, (((1,), (1,)), ((), ())), preferred_element_type=jnp.float32
    )


def expert_math(rows_in, rows_cot, row_gate, w_one, u_one, d_one):
    pre_gate = jnp.dot(rows_in, w_one, preferred_element_type=jnp.float32)
    pre_up = jnp.dot(rows_in, u_one, preferred_element_type=jnp.float32)
    sigma = jax.nn.sigmoid(pre_gate)
    active = pre_gate * sigma
    hidden = (active * pre_up).astype(jnp.bfloat16)
    back_hidden = contract_cols(rows_cot, d_one)
    expert_out = jnp.dot(hidden, d_one, preferred_element_type=jnp.float32)
    gate_term = jnp.sum(rows_cot.astype(jnp.float32) * expert_out, axis=1)
    weight_col = row_gate.astype(jnp.float32)[:, None]
    scaled_back = weight_col * back_hidden
    grad_pre_gate = (scaled_back * pre_up * sigma * (1.0 + pre_gate * (1.0 - sigma))).astype(
        jnp.bfloat16
    )
    grad_pre_up = (scaled_back * active).astype(jnp.bfloat16)
    scaled_hidden = (weight_col * active * pre_up).astype(jnp.bfloat16)
    row_grad = (contract_cols(grad_pre_gate, w_one) + contract_cols(grad_pre_up, u_one)).astype(
        jnp.bfloat16
    )
    return (row_grad, gate_term.astype(jnp.bfloat16), grad_pre_gate, grad_pre_up, scaled_hidden)


def dispatched(tokens, cotangent, expert_ids, gates, w_gate, w_up, w_down):
    token_count = tokens.shape[0]
    model_width = tokens.shape[1]
    top_count = expert_ids.shape[1]
    expert_count = lax.axis_size("expert") * lax.axis_size("dp")
    assigned = token_count * top_count
    slot_count = assigned // expert_count
    position = jnp.arange(assigned, dtype=jnp.int32)
    order = jnp.argsort(expert_ids.reshape(-1) * assigned + position)
    rank = jnp.zeros((assigned,), jnp.int32).at[order].set(position)
    source = order // top_count
    send_in = tokens[source].reshape(expert_count, slot_count, model_width)
    send_cot = cotangent[source].reshape(expert_count, slot_count, model_width)
    send_gate = gates.reshape(-1)[order].reshape(expert_count, slot_count)
    w_one = w_gate[0]
    u_one = w_up[0]
    d_one = w_down[0]
    rows_in = lax.all_to_all(send_in, ("expert", "dp"), split_axis=0, concat_axis=0, tiled=True)
    rows_cot = lax.all_to_all(send_cot, ("expert", "dp"), split_axis=0, concat_axis=0, tiled=True)
    row_gate = lax.all_to_all(send_gate, ("expert", "dp"), split_axis=0, concat_axis=0, tiled=True)
    senders = rows_in.shape[0]
    width_slots = rows_in.shape[1]
    outputs = expert_math(
        rows_in.reshape(-1, model_width),
        rows_cot.reshape(-1, model_width),
        row_gate.reshape(-1),
        w_one,
        u_one,
        d_one,
    )
    back_rows = lax.all_to_all(
        outputs[0].reshape(senders, width_slots, model_width),
        ("expert", "dp"),
        split_axis=0,
        concat_axis=0,
        tiled=True,
    )
    back_gate = lax.all_to_all(
        outputs[1].reshape(senders, width_slots),
        ("expert", "dp"),
        split_axis=0,
        concat_axis=0,
        tiled=True,
    )
    results = (
        back_rows,
        back_gate,
        rows_in,
        rows_cot,
        outputs[2].reshape(senders, width_slots, -1),
        outputs[3].reshape(senders, width_slots, -1),
        outputs[4].reshape(senders, width_slots, -1),
    )
    back_rows, back_gate, recv_in, recv_cot, grad_pre_gate, grad_pre_up, scaled_hidden = results
    recv_in = recv_in.reshape(-1, model_width)
    recv_cot = recv_cot.reshape(-1, model_width)
    grad_pre_gate = grad_pre_gate.reshape(assigned, -1)
    grad_pre_up = grad_pre_up.reshape(assigned, -1)
    scaled_hidden = scaled_hidden.reshape(assigned, -1)
    grad_w_gate = contract_rows(recv_in, grad_pre_gate).astype(jnp.bfloat16)
    grad_w_up = contract_rows(recv_in, grad_pre_up).astype(jnp.bfloat16)
    grad_w_down = contract_rows(scaled_hidden, recv_cot).astype(jnp.bfloat16)
    back_flat = back_rows.reshape(assigned, model_width)[rank]
    tokens_grad = jnp.sum(
        back_flat.reshape(token_count, top_count, model_width).astype(jnp.float32), axis=1
    )
    gates_grad = back_gate.reshape(-1)[rank].reshape(token_count, top_count)
    return (
        tokens_grad.astype(jnp.bfloat16),
        gates_grad,
        grad_w_gate[None],
        grad_w_up[None],
        grad_w_down[None],
    )

CORES = 2
ROW_TILE = 1024
FACTOR_ROWS = 128
PRODUCT_TILE = 1024
LANES = 128
HBM = pl.BlockSpec(memory_space=pltpu.HBM)
VMEM = pl.BlockSpec(memory_space=pltpu.VMEM)


def wait_for(copies):
    for copy in copies:
        copy.wait()


def tiles(count, size, body):
    @pl.loop(0, count // size)
    def _(i):
        body(pl.ds(pl.multiple_of(i * size, size), size))


def work_cost(rows, depth, width):
    return pl.CostEstimate(flops=24 * rows * depth * width, bytes_accessed=2 * rows * depth, transcendentals=0)


def step_kernel(lines, step, steps, passed, waited, token_count, model_width, f, *refs):
    refs = list(refs)
    take = lambda n: [refs.pop(0) for _ in range(n)]
    blocks, (pick_ref,) = take(lines), take(1)
    gate_w, up_w, down_w = take(CORES), take(CORES), take(CORES)
    if step:
        take(8)
    take(passed + waited)
    row_own, row_far = take(2)
    tok_all, cot_all = take(2)
    factor_all = take(6)
    mate_factors = take(1)[0] if step == steps - 1 else None
    take(passed)
    tok, cot, wg, wu, wd, pre_gate, pre_up, back, gg, gu = take(10)
    factors = take(6)
    in_sem, out_sem = take(2)
    rows = lines * token_count
    room = row_own.shape[1] - model_width

    slot = iter(range(64))
    copy_in = lambda src, dst: pltpu.make_async_copy(src, dst, in_sem.at[next(slot)])
    line_rows = [pl.ds(i * token_count, token_count) for i in range(lines)]
    columns = [pl.ds(e * f, f) for e in range(CORES)]
    padded = blocks[0].shape[1] - model_width
    first = [copy_in(blocks[i].at[:, pl.ds(0, model_width)], tok.at[line_rows[i]]) for i in range(lines)]
    first += [copy_in(gate_w[e], wg.at[:, columns[e]]) for e in range(CORES)]
    second = [copy_in(up_w[e], wu.at[:, columns[e]]) for e in range(CORES)]
    third = [copy_in(blocks[i].at[:, pl.ds(model_width, padded)], cot.at[line_rows[i]]) for i in range(lines)]
    third += [copy_in(down_w[e], wd.at[columns[e]]) for e in range(CORES)]
    for copy in first + second + third:
        copy.start()

    def gate_tile(c):
        pre_gate[:, c] = jnp.dot(tok[...], wg[:, c], preferred_element_type=jnp.float32)

    def up_tile(c):
        pre_up[:, c] = jnp.dot(tok[...], wu[:, c], preferred_element_type=jnp.float32)

    def back_tile(c):
        back[:, c] = contract_cols(cot[:, :model_width], wd[c, :])

    def factor_tile(line, r):
        gate_cols = jnp.dot(cot[r, model_width:], pick_ref[...], preferred_element_type=jnp.float32)
        sums = []
        for e in range(CORES):
            c = columns[e]
            gate, up, bh = pre_gate[r, c], pre_up[r, c], back[r, c]
            sigma = jax.nn.sigmoid(gate)
            active = gate * sigma
            prod = active * up
            hidden = prod.astype(jnp.bfloat16)
            sums.append(jnp.sum(hidden.astype(jnp.float32) * bh, axis=1, keepdims=True))
            weight = gate_cols[:, e : e + 1]
            scaled_back = weight * bh
            grad_gate = (scaled_back * up * sigma * (1.0 + gate * (1.0 - sigma))).astype(jnp.bfloat16)
            grad_up = (scaled_back * active).astype(jnp.bfloat16)
            gg[r, c] = grad_gate
            gu[r, c] = grad_up
            factors[e][r, :] = grad_gate
            factors[CORES + e][r, :] = grad_up
            factors[2 * CORES + e][r, :] = (weight * prod).astype(jnp.bfloat16)
        lane = lax.broadcasted_iota(jnp.int32, (sums[0].shape[0], room), 1)
        place = CORES * (step * lines + line)
        found = jnp.where(lane == place, sums[0], jnp.where(lane == place + 1, sums[1], 0.0))
        return found

    def own_terms(r):
        row_own[r, model_width:] = factor_tile(0, r)

    wait_for(first)
    tiles(CORES * f, CORES * f, gate_tile)
    wait_for(second)
    tiles(CORES * f, CORES * f, up_tile)
    wait_for(third)
    tiles(CORES * f, CORES * f, back_tile)
    tiles(token_count, FACTOR_ROWS, own_terms)
    for i in range(1, lines):

        @pl.loop(0, token_count // FACTOR_ROWS)
        def _(j):
            near = pl.ds(pl.multiple_of((i - 1) * token_count + j * FACTOR_ROWS, FACTOR_ROWS), FACTOR_ROWS)
            r = pl.ds(pl.multiple_of(i * token_count + j * FACTOR_ROWS, FACTOR_ROWS), FACTOR_ROWS)
            row_far[near, model_width:] = factor_tile(i, r).astype(jnp.bfloat16)

    at = pl.ds(step * rows, rows)
    outs = [(tok, tok_all), (cot.at[:, pl.ds(0, model_width)], cot_all)] + list(zip(factors, factor_all))
    pairs = [(a, b.at[at]) for a, b in outs]
    if mate_factors is not None:
        pairs += [(factors[CORES * i + 1], mate_factors.at[:, pl.ds(i * f, f)]) for i in range(3)]
    out_copies = [pltpu.make_async_copy(a, b, out_sem.at[i]) for i, (a, b) in enumerate(pairs)]
    for copy in out_copies:
        copy.start()

    def row_tile(c):
        grad = contract_cols(gg[...], wg[c, :]) + contract_cols(gu[...], wu[c, :])
        row_own[:, c] = grad[:token_count]
        row_far[:, c] = grad[token_count:].astype(jnp.bfloat16)

    tiles(model_width, ROW_TILE, row_tile)
    wait_for(out_copies)


def one_step(step, steps, blocks, pick, weights, held, passed=(), waited=()):
    lines = len(blocks)
    token_count = blocks[0].shape[0]
    model_width, f = weights[0].shape
    padded = blocks[0].shape[1] - model_width
    rows, wide = lines * token_count, CORES * f
    bf = jnp.bfloat16
    ins = [*blocks, pick, *weights, *held, *passed, *waited]
    whole = [jax.ShapeDtypeStruct((steps * rows, model_width), bf)] * 2
    whole += [jax.ShapeDtypeStruct((steps * rows, f), bf)] * 6
    out_shape = [
        jax.ShapeDtypeStruct((token_count, padded), jnp.float32),
        jax.ShapeDtypeStruct(((lines - 1) * token_count, padded), bf),
        *whole,
    ]
    if step == steps - 1:
        out_shape.append(jax.ShapeDtypeStruct((rows, 3 * f), bf))
    base = lines + 1 + len(weights)
    aliases = {base + i: 2 + i for i in range(len(held))}
    base += len(held)
    aliases |= {base + i: len(out_shape) + i for i in range(len(passed))}
    out_shape += [jax.ShapeDtypeStruct(value.shape, value.dtype) for value in passed]
    scratch = [pltpu.VMEM((rows, model_width), bf), pltpu.VMEM((rows, padded), bf)]
    scratch += [pltpu.VMEM((model_width, wide), bf)] * 2 + [pltpu.VMEM((wide, model_width), bf)]
    scratch += [pltpu.VMEM((rows, wide), jnp.float32)] * 3 + [pltpu.VMEM((rows, wide), bf)] * 2
    scratch += [pltpu.VMEM((rows, f), bf)] * 6
    scratch += [pltpu.SemaphoreType.DMA((2 * lines + 3 * CORES,)), pltpu.SemaphoreType.DMA((11,))]
    outs = pl.pallas_call(
        lambda *refs: step_kernel(lines, step, steps, len(passed), len(waited), token_count, model_width, f, *refs),
        out_shape=out_shape,
        in_specs=[HBM] * lines + [VMEM] + [HBM] * (len(ins) - lines - 1),
        out_specs=[VMEM] * 2 + [HBM] * (len(out_shape) - 2),
        scratch_shapes=scratch,
        input_output_aliases=aliases,
        compiler_params=pltpu.CompilerParams(vmem_limit_bytes=60 * 1024 * 1024),
        cost_estimate=work_cost(rows, model_width, 5 * wide),
    )(*ins)
    return outs[0], outs[1], list(outs[2:10]), outs[10:]


def mate_kernel(count, tok_ref, cot_ref, gate_ref, up_ref, hid_ref, out, tok, cot, pair, hid, sem):
    f = hid.shape[1]
    top = pl.ds(0, count)
    first = [(gate_ref, pair.at[:, pl.ds(0, f)]), (up_ref, pair.at[:, pl.ds(f, f)]), (tok_ref, tok)]
    moves = first + [(hid_ref, hid), (cot_ref, cot)]
    copies = [pltpu.make_async_copy(src.at[top], dst, sem.at[i]) for i, (src, dst) in enumerate(moves)]
    for copy in copies:
        copy.start()

    def pair_tile(c):
        out[: 2 * f, c] = contract_rows(pair[...], tok[:, c]).astype(jnp.bfloat16)

    def down_tile(c):
        out[2 * f :, c] = contract_rows(hid[...], cot[:, c]).astype(jnp.bfloat16)

    wait_for(copies[:3])
    tiles(tok.shape[1], PRODUCT_TILE, pair_tile)
    wait_for(copies[3:])
    tiles(tok.shape[1], PRODUCT_TILE, down_tile)


def mate_products(count, tok, cot, gate, up, hid):
    model_width, f = tok.shape[1], gate.shape[1]
    bf = jnp.bfloat16
    return pl.pallas_call(
        lambda *refs: mate_kernel(count, *refs),
        out_shape=jax.ShapeDtypeStruct((3 * f, model_width), bf),
        in_specs=[HBM] * 5,
        out_specs=VMEM,
        scratch_shapes=[
            pltpu.VMEM((count, model_width), bf),
            pltpu.VMEM((count, model_width), bf),
            pltpu.VMEM((count, 2 * f), bf),
            pltpu.VMEM((count, f), bf),
            pltpu.SemaphoreType.DMA((5,)),
        ],
        compiler_params=pltpu.CompilerParams(vmem_limit_bytes=60 * 1024 * 1024),
        cost_estimate=work_cost(count, model_width, 3 * f),
    )(tok, cot, gate, up, hid)


def finish_kernel(lines, tok_ref, cot_ref, gate_ref, up_ref, hid_ref, got_ref, factor_ref, *refs):
    far_blocks = refs[:lines]
    gate_out, up_out, down_out, tok, cot, pair, hid, got, sem = refs[lines + 1 :]
    rows, model_width = tok_ref.shape
    f = gate_ref.shape[1]
    token_count = far_blocks[0].shape[0]
    near, far = pl.ds(0, rows), pl.ds(rows, lines * token_count)
    line = [pl.ds(rows + i * token_count, token_count) for i in range(lines)]
    first = [(gate_ref, pair.at[near, pl.ds(0, f)]), (up_ref, pair.at[near, pl.ds(f, f)]), (tok_ref, tok.at[near])]
    first += [(factor_ref.at[:, pl.ds(0, 2 * f)], pair.at[far]), (got_ref, got)]
    first += [(far_blocks[i].at[:, pl.ds(0, model_width)], tok.at[line[i]]) for i in range(lines)]
    second = [(hid_ref, hid.at[near]), (factor_ref.at[:, pl.ds(2 * f, f)], hid.at[far]), (cot_ref, cot.at[near])]
    second += [(far_blocks[i].at[:, pl.ds(model_width, model_width)], cot.at[line[i]]) for i in range(lines)]
    copies = [pltpu.make_async_copy(src, dst, sem.at[i]) for i, (src, dst) in enumerate(first + second)]
    for copy in copies:
        copy.start()

    def pair_tile(c):
        both = contract_rows(pair[...], tok[:, c])
        both = (both + got[: 2 * f, c].astype(jnp.float32)).astype(jnp.bfloat16).T
        gate_out[c, :] = both[:, :f]
        up_out[c, :] = both[:, f:]

    def down_tile(c):
        down = contract_rows(hid[...], cot[:, c])
        down_out[:, c] = (down + got[2 * f :, c].astype(jnp.float32)).astype(jnp.bfloat16)

    wait_for(copies[: len(first)])
    tiles(model_width, PRODUCT_TILE, pair_tile)
    wait_for(copies[len(first) :])
    tiles(model_width, PRODUCT_TILE, down_tile)


def finish(tok, cot, gate, up, hid, got, far_factors, far_blocks, waited):
    rows, model_width = tok.shape
    f = gate.shape[1]
    lines = len(far_blocks)
    more = rows + lines * far_blocks[0].shape[0]
    bf = jnp.bfloat16
    ins = [tok, cot, gate, up, hid, got, far_factors, *far_blocks, waited]
    return pl.pallas_call(
        lambda *refs: finish_kernel(lines, *refs),
        out_shape=[jax.ShapeDtypeStruct((model_width, f), bf)] * 2 + [jax.ShapeDtypeStruct((f, model_width), bf)],
        in_specs=[HBM] * len(ins),
        out_specs=[VMEM] * 3,
        scratch_shapes=[
            pltpu.VMEM((more, model_width), bf),
            pltpu.VMEM((more, model_width), bf),
            pltpu.VMEM((more, 2 * f), bf),
            pltpu.VMEM((more, f), bf),
            pltpu.VMEM((3 * f, model_width), bf),
            pltpu.SemaphoreType.DMA((8 + 2 * lines,)),
        ],
        compiler_params=pltpu.CompilerParams(vmem_limit_bytes=60 * 1024 * 1024),
        cost_estimate=work_cost(more, model_width, 3 * f),
    )(*ins)


def pack_kernel(tok_ref, cot_ref, ids_ref, gates_ref, out, table, sem):
    model_width = tok_ref.shape[1]
    token_count, room = table.shape
    moves = [(tok_ref, 0, model_width), (cot_ref, model_width, model_width), (table, 2 * model_width, room)]
    copies = [
        pltpu.make_async_copy(src, out.at[:, pl.ds(start, width)], sem.at[i])
        for i, (src, start, width) in enumerate(moves)
    ]
    copies[0].start()
    copies[1].start()
    expert = lax.broadcasted_iota(jnp.int32, (room, token_count), 0)
    found = jnp.zeros((room, token_count), jnp.float32)
    for k in range(ids_ref.shape[0]):
        found = found + jnp.where(expert == ids_ref[k : k + 1, :], gates_ref[k : k + 1, :].astype(jnp.float32), 0.0)
    table[...] = found.T.astype(jnp.bfloat16)
    copies[2].start()
    wait_for(copies)


def pack(tokens, cotangent, expert_ids, gates, room):
    token_count, model_width = tokens.shape
    return pl.pallas_call(
        pack_kernel,
        out_shape=jax.ShapeDtypeStruct((token_count, 2 * model_width + room), jnp.bfloat16),
        in_specs=[VMEM, VMEM, VMEM, VMEM],
        out_specs=HBM,
        scratch_shapes=[pltpu.VMEM((token_count, room), jnp.bfloat16), pltpu.SemaphoreType.DMA((3,))],
        compiler_params=pltpu.CompilerParams(vmem_limit_bytes=60 * 1024 * 1024),
    )(tokens, cotangent, expert_ids.T, gates.T)


def gathered(tokens, cotangent, expert_ids, gates, w_gate, w_up, w_down):
    z_count = lax.axis_size("expert")
    dp_count = lax.axis_size("dp")
    x_count = dp_count // CORES
    expert_count = z_count * dp_count
    token_count, model_width = tokens.shape
    z_here = lax.axis_index("expert")
    dp_here = lax.axis_index("dp")

    def z_shift(value, step):
        return lax.ppermute(value, "expert", [(i, (i + step) % z_count) for i in range(z_count)])

    def x_shift(value, step):
        return lax.ppermute(value, "dp", [(i, (i + CORES * step) % dp_count) for i in range(dp_count)])

    def core_swap(value):
        return lax.ppermute(value, "dp", [(i, i ^ 1) for i in range(dp_count)])

    def after(value, *earlier):
        return lax.optimization_barrier((value, *earlier))[0]

    def across(block):
        return [block] + [x_shift(block, s) for s in range(1, x_count)]

    def home(d, carried=None):
        line = row_own[d]
        for s in range(1, x_count):
            line = line + x_shift(row_far[d][s - 1], x_count - s).astype(jnp.float32)
        if carried is not None:
            line = line + carried.astype(jnp.float32)
        return line.astype(jnp.bfloat16) if d else line

    table_width = -(-expert_count // LANES) * LANES
    block = pack(tokens, cotangent, expert_ids, gates, table_width)
    own_expert = z_here * dp_count + dp_here
    mate_expert = z_here * dp_count + (dp_here ^ 1)
    pick_row = jnp.arange(table_width, dtype=jnp.int32)[:, None]
    pick_column = jnp.arange(LANES, dtype=jnp.int32)[None, :]
    wanted = jnp.where(pick_column == 0, own_expert, mate_expert)
    pick = ((pick_row == wanted) & (pick_column < CORES)).astype(jnp.bfloat16)

    weights = []
    for own in (w_gate[0], w_up[0], w_down[0]):
        weights += [own, core_swap(own)]
    ring = z_shift(block, 1)
    pairs = [across(block)]
    ring = after(ring, *weights[1::2])

    row_own, row_far, held, line, carried = [], [], [], tokens, None
    mate = jnp.zeros((3 * w_gate.shape[2], model_width), jnp.bfloat16)
    for d in range(z_count):
        ready = []
        if d + 1 < z_count:
            if d > 1 and d + 2 == z_count:
                pairs.append([ring] + [z_shift(block, 1) for block in pairs[d][1:]])
            else:
                pairs.append(across(ring))
            following = z_shift(ring, 1) if d + 2 < z_count else None
            ready = [ring]
        passed, waited = [], []
        if d and d + 1 == z_count:
            count = d * x_count * token_count
            mate = mate_products(count, held[0], held[1], held[3], held[5], held[7])
            passed, waited = [row_far[0][0]], [mate]
            if d > 1:
                carried = home(1)
                waited.append(carried)
                carried = z_shift(carried, 1)
        outs = one_step(d, z_count, pairs[d], after(pick, *ready), weights, held, passed, waited)
        own, far, held, mate_factors = outs
        if len(mate_factors) > 1:
            row_far[0] = mate_factors[1][None]
        if d + 1 < z_count:
            far = after(far, pairs[d + 1][-1])
        if d + 2 < z_count:
            ring = after(following, far)
        row_own.append(own)
        row_far.append(far.reshape(x_count - 1, token_count, -1))

    for d in range(1 if carried is None else 2, z_count):
        line = home(d, carried)
        carried = z_shift(line, 1)
    got = core_swap(mate)
    far_blocks = [core_swap(block) for block in pairs[-1]]
    far_factors = core_swap(mate_factors[0])
    grads = finish(held[0], held[1], held[2], held[4], held[6], got, far_factors, far_blocks, line)

    row_own[0] = after(row_own[0], grads[0])
    total = home(0, carried)
    tokens_grad = total[:, :model_width].astype(jnp.bfloat16)
    back = total[:, model_width : model_width + expert_count]
    column_ids = []
    for d in range(z_count):
        for s in range(x_count):
            dp_from = (dp_here + CORES * s) % dp_count
            first = ((z_here + d) % z_count) * dp_count
            column_ids += [first + dp_from, first + (dp_from ^ 1)]
    same = expert_ids[:, :, None] == jnp.stack(column_ids)
    gates_grad = jnp.sum(jnp.where(same, back[:, None, :], 0.0), axis=2).astype(jnp.bfloat16)
    return (tokens_grad, gates_grad, *[g[None] for g in grads])


def per_device(tokens, cotangent, expert_ids, gates, w_gate, w_up, w_down):
    expert_count = lax.axis_size("expert") * lax.axis_size("dp")
    plan = gathered if expert_count <= 4 * expert_ids.shape[1] and lax.axis_size("dp") % CORES == 0 else dispatched
    return plan(tokens, cotangent, expert_ids, gates, w_gate, w_up, w_down)


def solution(mesh):
    placed = (
        P(("group", "expert", "dp"), None),
        P(("group", "expert", "dp"), None),
        P(("group", "expert", "dp"), None),
        P(("group", "expert", "dp"), None),
        P(("expert", "dp"), None, None),
        P(("expert", "dp"), None, None),
        P(("expert", "dp"), None, None),
    )
    return jax.shard_map(
        per_device,
        mesh=mesh,
        in_specs=placed,
        out_specs=(
            P(("group", "expert", "dp"), None),
            P(("group", "expert", "dp"), None),
            P(("group", "expert", "dp"), None, None),
            P(("group", "expert", "dp"), None, None),
            P(("group", "expert", "dp"), None, None),
        ),
        check_vma=False,
    )
```

```python
import jax
import jax.numpy as jnp
from jax import lax
from jax.experimental import pallas as pl
from jax.experimental.pallas import tpu as pltpu
from jax.sharding import PartitionSpec as P


def contract_rows(left, right):
    return lax.dot_general(
        left, right, (((0,), (0,)), ((), ())), preferred_element_type=jnp.float32
    )


def contract_cols(left, right):
    return lax.dot_general(
        left, right, (((1,), (1,)), ((), ())), preferred_element_type=jnp.float32
    )


def expert_math(rows_in, rows_cot, row_gate, w_one, u_one, d_one):
    pre_gate = jnp.dot(rows_in, w_one, preferred_element_type=jnp.float32)
    pre_up = jnp.dot(rows_in, u_one, preferred_element_type=jnp.float32)
    sigma = jax.nn.sigmoid(pre_gate)
    active = pre_gate * sigma
    hidden = (active * pre_up).astype(jnp.bfloat16)
    back_hidden = contract_cols(rows_cot, d_one)
    expert_out = jnp.dot(hidden, d_one, preferred_element_type=jnp.float32)
    gate_term = jnp.sum(rows_cot.astype(jnp.float32) * expert_out, axis=1)
    weight_col = row_gate.astype(jnp.float32)[:, None]
    scaled_back = weight_col * back_hidden
    grad_pre_gate = (scaled_back * pre_up * sigma * (1.0 + pre_gate * (1.0 - sigma))).astype(
        jnp.bfloat16
    )
    grad_pre_up = (scaled_back * active).astype(jnp.bfloat16)
    scaled_hidden = (weight_col * active * pre_up).astype(jnp.bfloat16)
    row_grad = (contract_cols(grad_pre_gate, w_one) + contract_cols(grad_pre_up, u_one)).astype(
        jnp.bfloat16
    )
    return (row_grad, gate_term.astype(jnp.bfloat16), grad_pre_gate, grad_pre_up, scaled_hidden)


def dispatched(tokens, cotangent, expert_ids, gates, w_gate, w_up, w_down):
    token_count = tokens.shape[0]
    model_width = tokens.shape[1]
    top_count = expert_ids.shape[1]
    expert_count = lax.axis_size("expert") * lax.axis_size("dp")
    assigned = token_count * top_count
    slot_count = assigned // expert_count
    position = jnp.arange(assigned, dtype=jnp.int32)
    order = jnp.argsort(expert_ids.reshape(-1) * assigned + position)
    rank = jnp.zeros((assigned,), jnp.int32).at[order].set(position)
    source = order // top_count
    send_in = tokens[source].reshape(expert_count, slot_count, model_width)
    send_cot = cotangent[source].reshape(expert_count, slot_count, model_width)
    send_gate = gates.reshape(-1)[order].reshape(expert_count, slot_count)
    w_one = w_gate[0]
    u_one = w_up[0]
    d_one = w_down[0]
    rows_in = lax.all_to_all(send_in, ("expert", "dp"), split_axis=0, concat_axis=0, tiled=True)
    rows_cot = lax.all_to_all(send_cot, ("expert", "dp"), split_axis=0, concat_axis=0, tiled=True)
    row_gate = lax.all_to_all(send_gate, ("expert", "dp"), split_axis=0, concat_axis=0, tiled=True)
    senders = rows_in.shape[0]
    width_slots = rows_in.shape[1]
    outputs = expert_math(
        rows_in.reshape(-1, model_width),
        rows_cot.reshape(-1, model_width),
        row_gate.reshape(-1),
        w_one,
        u_one,
        d_one,
    )
    back_rows = lax.all_to_all(
        outputs[0].reshape(senders, width_slots, model_width),
        ("expert", "dp"),
        split_axis=0,
        concat_axis=0,
        tiled=True,
    )
    back_gate = lax.all_to_all(
        outputs[1].reshape(senders, width_slots),
        ("expert", "dp"),
        split_axis=0,
        concat_axis=0,
        tiled=True,
    )
    results = (
        back_rows,
        back_gate,
        rows_in,
        rows_cot,
        outputs[2].reshape(senders, width_slots, -1),
        outputs[3].reshape(senders, width_slots, -1),
        outputs[4].reshape(senders, width_slots, -1),
    )
    back_rows, back_gate, recv_in, recv_cot, grad_pre_gate, grad_pre_up, scaled_hidden = results
    recv_in = recv_in.reshape(-1, model_width)
    recv_cot = recv_cot.reshape(-1, model_width)
    grad_pre_gate = grad_pre_gate.reshape(assigned, -1)
    grad_pre_up = grad_pre_up.reshape(assigned, -1)
    scaled_hidden = scaled_hidden.reshape(assigned, -1)
    grad_w_gate = contract_rows(recv_in, grad_pre_gate).astype(jnp.bfloat16)
    grad_w_up = contract_rows(recv_in, grad_pre_up).astype(jnp.bfloat16)
    grad_w_down = contract_rows(scaled_hidden, recv_cot).astype(jnp.bfloat16)
    back_flat = back_rows.reshape(assigned, model_width)[rank]
    tokens_grad = jnp.sum(
        back_flat.reshape(token_count, top_count, model_width).astype(jnp.float32), axis=1
    )
    gates_grad = back_gate.reshape(-1)[rank].reshape(token_count, top_count)
    return (
        tokens_grad.astype(jnp.bfloat16),
        gates_grad,
        grad_w_gate[None],
        grad_w_up[None],
        grad_w_down[None],
    )

CORES = 2
ROW_TILE = 1024
FACTOR_ROWS = 128
PRODUCT_TILE = 1024
LANES = 128
HBM = pl.BlockSpec(memory_space=pltpu.HBM)
VMEM = pl.BlockSpec(memory_space=pltpu.VMEM)


def wait_for(copies):
    for copy in copies:
        copy.wait()


def tiles(count, size, body):
    @pl.loop(0, count // size)
    def _(i):
        body(pl.ds(pl.multiple_of(i * size, size), size))


def work_cost(rows, depth, width):
    return pl.CostEstimate(flops=12 * rows * depth * width, bytes_accessed=2 * rows * depth, transcendentals=0)


def step_kernel(lines, step, steps, passed, waited, token_count, model_width, f, *refs):
    refs = list(refs)
    take = lambda n: [refs.pop(0) for _ in range(n)]
    blocks, (pick_ref,) = take(lines), take(1)
    gate_w, up_w, down_w = take(CORES), take(CORES), take(CORES)
    if step:
        take(8)
    take(passed + waited)
    row_own, row_far = take(2)
    tok_all, cot_all = take(2)
    factor_all = take(6)
    mate_factors = take(1)[0] if step == steps - 1 else None
    take(passed)
    tok, cot, wg, wu, wd, pre_gate, pre_up, back, gg, gu = take(10)
    factors = take(6)
    in_sem, out_sem = take(2)
    rows = lines * token_count
    room = row_own.shape[1] - model_width

    slot = iter(range(64))
    copy_in = lambda src, dst: pltpu.make_async_copy(src, dst, in_sem.at[next(slot)])
    line_rows = [pl.ds(i * token_count, token_count) for i in range(lines)]
    columns = [pl.ds(e * f, f) for e in range(CORES)]
    padded = blocks[0].shape[1] - model_width
    first = [copy_in(blocks[i].at[:, pl.ds(0, model_width)], tok.at[line_rows[i]]) for i in range(lines)]
    first += [copy_in(gate_w[e], wg.at[:, columns[e]]) for e in range(CORES)]
    second = [copy_in(up_w[e], wu.at[:, columns[e]]) for e in range(CORES)]
    third = [copy_in(blocks[i].at[:, pl.ds(model_width, padded)], cot.at[line_rows[i]]) for i in range(lines)]
    third += [copy_in(down_w[e], wd.at[columns[e]]) for e in range(CORES)]
    for copy in first + second + third:
        copy.start()

    def gate_tile(c):
        pre_gate[:, c] = jnp.dot(tok[...], wg[:, c], preferred_element_type=jnp.float32)

    def up_tile(c):
        pre_up[:, c] = jnp.dot(tok[...], wu[:, c], preferred_element_type=jnp.float32)

    def back_tile(c):
        back[:, c] = contract_cols(cot[:, :model_width], wd[c, :])

    def factor_tile(line, r):
        gate_cols = jnp.dot(cot[r, model_width:], pick_ref[...], preferred_element_type=jnp.float32)
        sums = []
        for e in range(CORES):
            c = columns[e]
            gate, up, bh = pre_gate[r, c], pre_up[r, c], back[r, c]
            sigma = jax.nn.sigmoid(gate)
            active = gate * sigma
            prod = active * up
            hidden = prod.astype(jnp.bfloat16)
            sums.append(jnp.sum(hidden.astype(jnp.float32) * bh, axis=1, keepdims=True))
            weight = gate_cols[:, e : e + 1]
            scaled_back = weight * bh
            grad_gate = (scaled_back * up * sigma * (1.0 + gate * (1.0 - sigma))).astype(jnp.bfloat16)
            grad_up = (scaled_back * active).astype(jnp.bfloat16)
            gg[r, c] = grad_gate
            gu[r, c] = grad_up
            factors[e][r, :] = grad_gate
            factors[CORES + e][r, :] = grad_up
            factors[2 * CORES + e][r, :] = (weight * prod).astype(jnp.bfloat16)
        lane = lax.broadcasted_iota(jnp.int32, (sums[0].shape[0], room), 1)
        place = CORES * (step * lines + line)
        found = jnp.where(lane == place, sums[0], jnp.where(lane == place + 1, sums[1], 0.0))
        return found

    def own_terms(r):
        row_own[r, model_width:] = factor_tile(0, r)

    wait_for(first)
    tiles(CORES * f, CORES * f, gate_tile)
    wait_for(second)
    tiles(CORES * f, CORES * f, up_tile)
    wait_for(third)
    tiles(CORES * f, CORES * f, back_tile)
    tiles(token_count, FACTOR_ROWS, own_terms)
    for i in range(1, lines):

        @pl.loop(0, token_count // FACTOR_ROWS)
        def _(j):
            near = pl.ds(pl.multiple_of((i - 1) * token_count + j * FACTOR_ROWS, FACTOR_ROWS), FACTOR_ROWS)
            r = pl.ds(pl.multiple_of(i * token_count + j * FACTOR_ROWS, FACTOR_ROWS), FACTOR_ROWS)
            row_far[near, model_width:] = factor_tile(i, r).astype(jnp.bfloat16)

    at = pl.ds(step * rows, rows)
    outs = [(tok, tok_all), (cot.at[:, pl.ds(0, model_width)], cot_all)] + list(zip(factors, factor_all))
    pairs = [(a, b.at[at]) for a, b in outs]
    if mate_factors is not None:
        pairs += [(factors[CORES * i + 1], mate_factors.at[:, pl.ds(i * f, f)]) for i in range(3)]
    out_copies = [pltpu.make_async_copy(a, b, out_sem.at[i]) for i, (a, b) in enumerate(pairs)]
    for copy in out_copies:
        copy.start()

    def row_tile(c):
        grad = contract_cols(gg[...], wg[c, :]) + contract_cols(gu[...], wu[c, :])
        row_own[:, c] = grad[:token_count]
        row_far[:, c] = grad[token_count:].astype(jnp.bfloat16)

    tiles(model_width, ROW_TILE, row_tile)
    wait_for(out_copies)


def one_step(step, steps, blocks, pick, weights, held, passed=(), waited=()):
    lines = len(blocks)
    token_count = blocks[0].shape[0]
    model_width, f = weights[0].shape
    padded = blocks[0].shape[1] - model_width
    rows, wide = lines * token_count, CORES * f
    bf = jnp.bfloat16
    ins = [*blocks, pick, *weights, *held, *passed, *waited]
    whole = [jax.ShapeDtypeStruct((steps * rows, model_width), bf)] * 2
    whole += [jax.ShapeDtypeStruct((steps * rows, f), bf)] * 6
    out_shape = [
        jax.ShapeDtypeStruct((token_count, padded), jnp.float32),
        jax.ShapeDtypeStruct(((lines - 1) * token_count, padded), bf),
        *whole,
    ]
    if step == steps - 1:
        out_shape.append(jax.ShapeDtypeStruct((rows, 3 * f), bf))
    base = lines + 1 + len(weights)
    aliases = {base + i: 2 + i for i in range(len(held))}
    base += len(held)
    aliases |= {base + i: len(out_shape) + i for i in range(len(passed))}
    out_shape += [jax.ShapeDtypeStruct(value.shape, value.dtype) for value in passed]
    scratch = [pltpu.VMEM((rows, model_width), bf), pltpu.VMEM((rows, padded), bf)]
    scratch += [pltpu.VMEM((model_width, wide), bf)] * 2 + [pltpu.VMEM((wide, model_width), bf)]
    scratch += [pltpu.VMEM((rows, wide), jnp.float32)] * 3 + [pltpu.VMEM((rows, wide), bf)] * 2
    scratch += [pltpu.VMEM((rows, f), bf)] * 6
    scratch += [pltpu.SemaphoreType.DMA((2 * lines + 3 * CORES,)), pltpu.SemaphoreType.DMA((11,))]
    outs = pl.pallas_call(
        lambda *refs: step_kernel(lines, step, steps, len(passed), len(waited), token_count, model_width, f, *refs),
        out_shape=out_shape,
        in_specs=[HBM] * lines + [VMEM] + [HBM] * (len(ins) - lines - 1),
        out_specs=[VMEM] * 2 + [HBM] * (len(out_shape) - 2),
        scratch_shapes=scratch,
        input_output_aliases=aliases,
        compiler_params=pltpu.CompilerParams(vmem_limit_bytes=60 * 1024 * 1024),
        cost_estimate=work_cost(rows, model_width, 5 * wide),
    )(*ins)
    return outs[0], outs[1], list(outs[2:10]), outs[10:]


def mate_kernel(count, tok_ref, cot_ref, gate_ref, up_ref, hid_ref, out, tok, cot, pair, hid, sem):
    f = hid.shape[1]
    top = pl.ds(0, count)
    first = [(gate_ref, pair.at[:, pl.ds(0, f)]), (up_ref, pair.at[:, pl.ds(f, f)]), (tok_ref, tok)]
    moves = first + [(hid_ref, hid), (cot_ref, cot)]
    copies = [pltpu.make_async_copy(src.at[top], dst, sem.at[i]) for i, (src, dst) in enumerate(moves)]
    for copy in copies:
        copy.start()

    def pair_tile(c):
        out[: 2 * f, c] = contract_rows(pair[...], tok[:, c]).astype(jnp.bfloat16)

    def down_tile(c):
        out[2 * f :, c] = contract_rows(hid[...], cot[:, c]).astype(jnp.bfloat16)

    wait_for(copies[:3])
    tiles(tok.shape[1], PRODUCT_TILE, pair_tile)
    wait_for(copies[3:])
    tiles(tok.shape[1], PRODUCT_TILE, down_tile)


def mate_products(count, tok, cot, gate, up, hid):
    model_width, f = tok.shape[1], gate.shape[1]
    bf = jnp.bfloat16
    return pl.pallas_call(
        lambda *refs: mate_kernel(count, *refs),
        out_shape=jax.ShapeDtypeStruct((3 * f, model_width), bf),
        in_specs=[HBM] * 5,
        out_specs=VMEM,
        scratch_shapes=[
            pltpu.VMEM((count, model_width), bf),
            pltpu.VMEM((count, model_width), bf),
            pltpu.VMEM((count, 2 * f), bf),
            pltpu.VMEM((count, f), bf),
            pltpu.SemaphoreType.DMA((5,)),
        ],
        compiler_params=pltpu.CompilerParams(vmem_limit_bytes=60 * 1024 * 1024),
        cost_estimate=work_cost(count, model_width, 3 * f),
    )(tok, cot, gate, up, hid)


def finish_kernel(lines, tok_ref, cot_ref, gate_ref, up_ref, hid_ref, got_ref, factor_ref, *refs):
    far_blocks = refs[:lines]
    gate_out, up_out, down_out, tok, cot, pair, hid, got, sem = refs[lines + 1 :]
    rows, model_width = tok_ref.shape
    f = gate_ref.shape[1]
    token_count = far_blocks[0].shape[0]
    near, far = pl.ds(0, rows), pl.ds(rows, lines * token_count)
    line = [pl.ds(rows + i * token_count, token_count) for i in range(lines)]
    first = [(gate_ref, pair.at[near, pl.ds(0, f)]), (up_ref, pair.at[near, pl.ds(f, f)]), (tok_ref, tok.at[near])]
    first += [(factor_ref.at[:, pl.ds(0, 2 * f)], pair.at[far]), (got_ref, got)]
    first += [(far_blocks[i].at[:, pl.ds(0, model_width)], tok.at[line[i]]) for i in range(lines)]
    second = [(hid_ref, hid.at[near]), (factor_ref.at[:, pl.ds(2 * f, f)], hid.at[far]), (cot_ref, cot.at[near])]
    second += [(far_blocks[i].at[:, pl.ds(model_width, model_width)], cot.at[line[i]]) for i in range(lines)]
    copies = [pltpu.make_async_copy(src, dst, sem.at[i]) for i, (src, dst) in enumerate(first + second)]
    for copy in copies:
        copy.start()

    def pair_tile(c):
        both = contract_rows(pair[...], tok[:, c])
        both = (both + got[: 2 * f, c].astype(jnp.float32)).astype(jnp.bfloat16).T
        gate_out[c, :] = both[:, :f]
        up_out[c, :] = both[:, f:]

    def down_tile(c):
        down = contract_rows(hid[...], cot[:, c])
        down_out[:, c] = (down + got[2 * f :, c].astype(jnp.float32)).astype(jnp.bfloat16)

    wait_for(copies[: len(first)])
    tiles(model_width, PRODUCT_TILE, pair_tile)
    wait_for(copies[len(first) :])
    tiles(model_width, PRODUCT_TILE, down_tile)


def finish(tok, cot, gate, up, hid, got, far_factors, far_blocks, waited):
    rows, model_width = tok.shape
    f = gate.shape[1]
    lines = len(far_blocks)
    more = rows + lines * far_blocks[0].shape[0]
    bf = jnp.bfloat16
    ins = [tok, cot, gate, up, hid, got, far_factors, *far_blocks, waited]
    return pl.pallas_call(
        lambda *refs: finish_kernel(lines, *refs),
        out_shape=[jax.ShapeDtypeStruct((model_width, f), bf)] * 2 + [jax.ShapeDtypeStruct((f, model_width), bf)],
        in_specs=[HBM] * len(ins),
        out_specs=[VMEM] * 3,
        scratch_shapes=[
            pltpu.VMEM((more, model_width), bf),
            pltpu.VMEM((more, model_width), bf),
            pltpu.VMEM((more, 2 * f), bf),
            pltpu.VMEM((more, f), bf),
            pltpu.VMEM((3 * f, model_width), bf),
            pltpu.SemaphoreType.DMA((8 + 2 * lines,)),
        ],
        compiler_params=pltpu.CompilerParams(vmem_limit_bytes=60 * 1024 * 1024),
        cost_estimate=work_cost(more, model_width, 3 * f),
    )(*ins)


def pack_kernel(tok_ref, cot_ref, ids_ref, gates_ref, out, table, sem):
    model_width = tok_ref.shape[1]
    token_count, room = table.shape
    moves = [(tok_ref, 0, model_width), (cot_ref, model_width, model_width), (table, 2 * model_width, room)]
    copies = [
        pltpu.make_async_copy(src, out.at[:, pl.ds(start, width)], sem.at[i])
        for i, (src, start, width) in enumerate(moves)
    ]
    copies[0].start()
    copies[1].start()
    expert = lax.broadcasted_iota(jnp.int32, (room, token_count), 0)
    found = jnp.zeros((room, token_count), jnp.float32)
    for k in range(ids_ref.shape[0]):
        found = found + jnp.where(expert == ids_ref[k : k + 1, :], gates_ref[k : k + 1, :].astype(jnp.float32), 0.0)
    table[...] = found.T.astype(jnp.bfloat16)
    copies[2].start()
    wait_for(copies)


def pack(tokens, cotangent, expert_ids, gates, room):
    token_count, model_width = tokens.shape
    return pl.pallas_call(
        pack_kernel,
        out_shape=jax.ShapeDtypeStruct((token_count, 2 * model_width + room), jnp.bfloat16),
        in_specs=[VMEM, VMEM, VMEM, VMEM],
        out_specs=HBM,
        scratch_shapes=[pltpu.VMEM((token_count, room), jnp.bfloat16), pltpu.SemaphoreType.DMA((3,))],
        compiler_params=pltpu.CompilerParams(vmem_limit_bytes=60 * 1024 * 1024),
    )(tokens, cotangent, expert_ids.T, gates.T)


def gathered(tokens, cotangent, expert_ids, gates, w_gate, w_up, w_down):
    z_count = lax.axis_size("expert")
    dp_count = lax.axis_size("dp")
    x_count = dp_count // CORES
    expert_count = z_count * dp_count
    token_count, model_width = tokens.shape
    z_here = lax.axis_index("expert")
    dp_here = lax.axis_index("dp")

    def z_shift(value, step):
        return lax.ppermute(value, "expert", [(i, (i + step) % z_count) for i in range(z_count)])

    def x_shift(value, step):
        return lax.ppermute(value, "dp", [(i, (i + CORES * step) % dp_count) for i in range(dp_count)])

    def core_swap(value):
        return lax.ppermute(value, "dp", [(i, i ^ 1) for i in range(dp_count)])

    def after(value, *earlier):
        return lax.optimization_barrier((value, *earlier))[0]

    def across(block):
        return [block] + [x_shift(block, s) for s in range(1, x_count)]

    def home(d, carried=None):
        line = row_own[d]
        for s in range(1, x_count):
            line = line + x_shift(row_far[d][s - 1], x_count - s).astype(jnp.float32)
        if carried is not None:
            line = line + carried.astype(jnp.float32)
        return line.astype(jnp.bfloat16) if d else line

    table_width = -(-expert_count // LANES) * LANES
    block = pack(tokens, cotangent, expert_ids, gates, table_width)
    own_expert = z_here * dp_count + dp_here
    mate_expert = z_here * dp_count + (dp_here ^ 1)
    pick_row = jnp.arange(table_width, dtype=jnp.int32)[:, None]
    pick_column = jnp.arange(LANES, dtype=jnp.int32)[None, :]
    wanted = jnp.where(pick_column == 0, own_expert, mate_expert)
    pick = ((pick_row == wanted) & (pick_column < CORES)).astype(jnp.bfloat16)

    weights = []
    for own in (w_gate[0], w_up[0], w_down[0]):
        weights += [own, core_swap(own)]
    ring = z_shift(block, 1)
    pairs = [across(block)]
    ring = after(ring, *weights[1::2])

    row_own, row_far, held, line, carried = [], [], [], tokens, None
    mate = jnp.zeros((3 * w_gate.shape[2], model_width), jnp.bfloat16)
    for d in range(z_count):
        ready = []
        if d + 1 < z_count:
            if d > 1 and d + 2 == z_count:
                pairs.append([ring] + [z_shift(block, 1) for block in pairs[d][1:]])
            else:
                pairs.append(across(ring))
            following = z_shift(ring, 1) if d + 2 < z_count else None
            ready = [ring]
        passed, waited = [], []
        if d and d + 1 == z_count:
            count = d * x_count * token_count
            mate = mate_products(count, held[0], held[1], held[3], held[5], held[7])
            passed, waited = [row_far[0][0]], [mate]
            if d > 1:
                carried = home(1)
                waited.append(carried)
                carried = z_shift(carried, 1)
        outs = one_step(d, z_count, pairs[d], after(pick, *ready), weights, held, passed, waited)
        own, far, held, mate_factors = outs
        if len(mate_factors) > 1:
            row_far[0] = mate_factors[1][None]
        if d + 1 < z_count:
            far = after(far, pairs[d + 1][-1])
        if d + 2 < z_count:
            ring = after(following, far)
        row_own.append(own)
        row_far.append(far.reshape(x_count - 1, token_count, -1))

    for d in range(1 if carried is None else 2, z_count):
        line = home(d, carried)
        carried = z_shift(line, 1)
    got = core_swap(mate)
    far_blocks = [core_swap(block) for block in pairs[-1]]
    far_factors = core_swap(mate_factors[0])
    grads = finish(held[0], held[1], held[2], held[4], held[6], got, far_factors, far_blocks, line)

    row_own[0] = after(row_own[0], grads[0])
    total = home(0, carried)
    tokens_grad = total[:, :model_width].astype(jnp.bfloat16)
    back = total[:, model_width : model_width + expert_count]
    column_ids = []
    for d in range(z_count):
        for s in range(x_count):
            dp_from = (dp_here + CORES * s) % dp_count
            first = ((z_here + d) % z_count) * dp_count
            column_ids += [first + dp_from, first + (dp_from ^ 1)]
    same = expert_ids[:, :, None] == jnp.stack(column_ids)
    gates_grad = jnp.sum(jnp.where(same, back[:, None, :], 0.0), axis=2).astype(jnp.bfloat16)
    return (tokens_grad, gates_grad, *[g[None] for g in grads])


def per_device(tokens, cotangent, expert_ids, gates, w_gate, w_up, w_down):
    expert_count = lax.axis_size("expert") * lax.axis_size("dp")
    plan = gathered if expert_count <= 4 * expert_ids.shape[1] and lax.axis_size("dp") % CORES == 0 else dispatched
    return plan(tokens, cotangent, expert_ids, gates, w_gate, w_up, w_down)


def solution(mesh):
    placed = (
        P(("group", "expert", "dp"), None),
        P(("group", "expert", "dp"), None),
        P(("group", "expert", "dp"), None),
        P(("group", "expert", "dp"), None),
        P(("expert", "dp"), None, None),
        P(("expert", "dp"), None, None),
        P(("expert", "dp"), None, None),
    )
    return jax.shard_map(
        per_device,
        mesh=mesh,
        in_specs=placed,
        out_specs=(
            P(("group", "expert", "dp"), None),
            P(("group", "expert", "dp"), None),
            P(("group", "expert", "dp"), None, None),
            P(("group", "expert", "dp"), None, None),
            P(("group", "expert", "dp"), None, None),
        ),
        check_vma=False,
    )
```
